256 devices in a mesh: proto: 64 (over y, z, core), batch: 4 (over x).
Axes of the slice: x: 4, y: 4, z: 8, core: 2. Of those that a mesh axis runs over, the one named last changes fastest.
Arguments:
- features: bfloat16 [2, 4096, 1024], P(None, 'batch', 'proto'), may hold values from -240 to 240
- prototypes: bfloat16 [1024, 65536], P(None, 'proto'), may hold values from -1.5 to 1.5
Outputs:
- proto_grad: float32 [1024, 65536], P('batch', 'proto')
- loss_value: float32 [], replicated
The draws below stay inside these ranges and needn't reach their ends.
All inputs are finite; a program needn't handle non-finite values.
Results may differ from the reference program's by a relative error of at most 0.003.
Values may be sent and summed in bfloat16 or wider, within the bound.
A program may use at most 64 MiB of HBM per device.

```python
import math
import jax
import jax.numpy as jnp
from jax import lax

D = 1024
ITERS = 3
K = 65536
ROWS = 4096


def shared_centers(key):
    groups = max(ROWS // 16, 4)
    return jnp.clip(jax.random.normal(jax.random.fold_in(key, 5), (D, groups), jnp.float32), -5.0, 5.0)


def draw_prototypes(key, part):
    centers = shared_centers(key)
    groups = centers.shape[1]
    key = jax.random.fold_in(key, 11)
    own_key, limit_key, member_key, align_key, scale_key = jax.random.split(key, 5)
    own_part = jnp.clip(jax.random.normal(own_key, (D, K), jnp.float32), -5.0, 5.0)
    limits = jax.random.randint(limit_key, (K,), 1, groups + 1)
    member = groups - 1 - jax.random.randint(member_key, (K,), 0, limits)
    position = jnp.arange(K, dtype=jnp.float32) / K
    alignment = 0.45 + 0.3 * position + 0.17 * jax.random.uniform(align_key, (K,), jnp.float32)
    spread = 4.0
    shared_part = jnp.take(centers, member, axis=1)
    directions = alignment[None, :] * shared_part + jnp.sqrt(1.0 - alignment * alignment)[None, :] * own_part
    column_scale = jnp.exp(jax.random.uniform(scale_key, (K,), jnp.float32) * math.log(spread))
    values = jnp.clip(directions * column_scale[None, :] * D ** (-0.5), -1.5, 1.5)
    return values.astype(jnp.bfloat16)


def draw_features(key, part):
    centers = shared_centers(key)
    groups = centers.shape[1]
    key = jax.random.fold_in(key, 12)
    pick_key, strength_key, noise_key, scale_key = jax.random.split(key, 4)
    member = jax.random.randint(pick_key, (ROWS,), 0, groups)
    rising = 1.0 + 1.5 * jnp.arange(ROWS, dtype=jnp.float32) / ROWS
    strength = jnp.exp(jax.random.uniform(strength_key, (2, ROWS), jnp.float32, math.log(0.35), math.log(2.0))) * rising[None, :]
    noise_part = jnp.clip(jax.random.normal(noise_key, (2, ROWS, D), jnp.float32), -5.0, 5.0)
    spread = 4.0
    sample_rescaling = jnp.exp(jax.random.uniform(scale_key, (2, ROWS), jnp.float32) * math.log(spread))
    aligned = jnp.take(centers, member, axis=1).T
    mixed = sample_rescaling[:, :, None] * (noise_part + strength[:, :, None] * aligned[None, :, :])
    return jnp.clip(mixed, -240.0, 240.0).astype(jnp.bfloat16)


def setup_inputs(seed: int = 0) -> dict:
    key_of = jax.random.split(jax.random.key(seed), 3)
    return {
        "features": draw_features(jax.random.fold_in(key_of[2], 71), 0),
        "prototypes": draw_prototypes(jax.random.fold_in(key_of[2], 71), 0),
    }


eps_assign = 0.05
heat_parameter = 0.1

def normalizer(values, along):
    return lax.rsqrt(lax.optimization_barrier(jnp.sum(values * values, axis=along)) + 1e-06)

def reference(features, prototypes):
    highest = lax.Precision.HIGHEST
    proto_wide = prototypes.astype(jnp.float32)
    proto_scale = normalizer(proto_wide, 0)
    unit_wide = proto_wide * proto_scale[None, :]
    unit_protos = unit_wide.astype(jnp.bfloat16)
    centroid_affinity_matrix = []
    instance_scale_factors = []
    for active_patch_position in range(2):
        raw_scores = jnp.dot(features[active_patch_position], unit_protos, preferred_element_type=jnp.float32)
        sample_rescaling = normalizer(features[active_patch_position].astype(jnp.float32), 1)
        instance_scale_factors.append(sample_rescaling)
        centroid_affinity_matrix.append(raw_scores * sample_rescaling[:, None])
    proto_factors = []
    sample_factors = []
    centroid_mass_vector = []
    for active_patch_position in range(2):
        sample_factor = jnp.ones((ROWS,), jnp.float32)
        proto_factor = jnp.ones((K,), jnp.float32)
        for iteration in range(ITERS):
            proto_factor = 1.0 / jnp.dot(sample_factor, jnp.exp(centroid_affinity_matrix[active_patch_position] / eps_assign), precision=highest)
            sample_factor = 1.0 / jnp.dot(jnp.exp(centroid_affinity_matrix[active_patch_position] / eps_assign), proto_factor, precision=highest)
        proto_factors.append(proto_factor)
        sample_factors.append(sample_factor)
        centroid_mass_vector.append(lax.optimization_barrier(jnp.sum(jnp.exp(centroid_affinity_matrix[active_patch_position] / heat_parameter), axis=1)))
    loss_sum = jnp.float32(0.0)
    grads = []
    for active_patch_position in range(2):
        other = 1 - active_patch_position
        partner_patch_membership = jnp.exp(centroid_affinity_matrix[other] / eps_assign) * proto_factors[other][None, :] * sample_factors[other][:, None]
        logarithmic_probabilities = centroid_affinity_matrix[active_patch_position] / heat_parameter - jnp.log(centroid_mass_vector[active_patch_position])[:, None]
        loss_sum = loss_sum + jnp.sum(partner_patch_membership * logarithmic_probabilities)
        estimated_membership = jnp.exp(centroid_affinity_matrix[active_patch_position] / heat_parameter) / centroid_mass_vector[active_patch_position][:, None]
        affinity_slope_matrix = ((estimated_membership - partner_patch_membership) / heat_parameter * instance_scale_factors[active_patch_position][:, None]).astype(jnp.bfloat16)
        grads.append(jnp.dot(features[active_patch_position].T, affinity_slope_matrix, preferred_element_type=jnp.float32))
    loss_value = -loss_sum / (2.0 * ROWS)
    proto_delta = grads[0] + grads[1]
    inner_sums = lax.optimization_barrier(jnp.sum(unit_wide * proto_delta, axis=0))
    proto_grad = proto_scale[None, :] * (proto_delta - unit_wide * inner_sums[None, :])
    return (proto_grad, loss_value)
```

```python
import functools
import math

import jax
import jax.numpy as jnp
from jax import lax
from jax.experimental import pallas as pl
from jax.experimental.pallas import tpu as pltpu
from jax.sharding import PartitionSpec as P

ITERS = 3
NX, NY, NZ, NC = 4, 4, 8, 2
VIEWS = 2
D = 1024
KD = 1024
RD = 1024
ROWS = NX * RD
PIECE = 16
CHUNK = 256
CHUNKS = KD // CHUNK
HEAT = 10.0
EXP2_SCALE = 10.0 * math.log2(math.e)
F32 = jnp.float32
BF16 = jnp.bfloat16
NT = (((1,), (1,)), ((), ()))


def kernel(feat_ref, proto_ref, grad_ref, loss_ref, ft, pv, ut, sc, kn, sg, scale, rscale, tot, part, xbuf, ybuf, zbuf,
           lx, ly, lz, inner, snd2, sndp, sndm, r1p, r1m, recp, recm, dp, dm, down,
           in_sem, z_s, z_r, y_s, y_r, f_s, f_r, c_s, c_r, xs_s, xs_r, ys_s, ys_r, zs_s, zs_r,
           lx_s, lx_r, ly_s, ly_r, lz_s, lz_r, in_s, in_r, h_s, h_r, d_s, d_r, e_s, e_r):
    xi = lax.axis_index("batch")
    me = lax.axis_index("proto")
    c = lax.rem(me, NC)
    z = lax.rem(lax.div(me, NC), NZ)
    y = lax.div(me, NC * NZ)

    def at_y(dy):
        return lax.rem(y + dy % NY, NY)

    def at_z(dz):
        return lax.rem(z + dz % NZ, NZ)

    def at_x(dx):
        return lax.rem(xi + dx % NX, NX)

    def dev(dx=0, dy=0, dz=0, dc=0):
        return ((at_y(dy) * NZ + at_z(dz)) * NC + lax.rem(c + dc, NC), at_x(dx))

    yc_peers = [(dy, dc) for dy in range(NY) for dc in range(NC) if dy or dc]
    z_order = [1, 7, 2, 6, 3, 5, 4]

    load_p = pltpu.make_async_copy(proto_ref, pv, in_sem.at[0])
    load_p.start()
    load_f = pltpu.make_async_copy(feat_ref, ft.at[:, y, z, c], in_sem.at[1])
    load_f.start()

    barrier = pltpu.get_barrier_semaphore()
    peers = [dev(dy=dy, dc=dc) for dy, dc in yc_peers]
    peers += [dev(dz=dz) for dz in z_order] + [dev(dx=dx) for dx in (1, 2, 3)]
    for peer in peers:
        pl.semaphore_signal(barrier, inc=1, device_id=peer, device_id_type=pl.DeviceIdType.MESH)

    load_p.wait()

    def square_step(i, acc):
        v = pv[pl.ds(pl.multiple_of(i * 16, 16), 16), :].astype(F32)
        return acc + v * v

    sq = lax.fori_loop(0, D // 16, square_step, jnp.zeros((16, KD), F32))
    scale[...] = lax.rsqrt(jnp.sum(sq, axis=0, keepdims=True) + 1e-6)

    def unit_step(i, _):
        rows = pl.ds(pl.multiple_of(i * 128, 128), 128)
        for kb in range(KD // 128):
            cols = slice(kb * 128, kb * 128 + 128)
            ut[cols, rows] = (pv[rows, cols].astype(F32) * scale[:, cols]).T.astype(BF16)
        return 0

    lax.fori_loop(0, D // 128, unit_step, 0)
    load_f.wait()
    pl.semaphore_wait(barrier, len(peers))

    sends = []

    def copy(src, dst, ssem, rsem, to):
        return pltpu.make_async_remote_copy(
            src_ref=src, dst_ref=dst, send_sem=ssem, recv_sem=rsem, device_id=to, device_id_type=pl.DeviceIdType.MESH
        )

    def send(src, dst, ssem, rsem, to):
        cp = copy(src, dst, ssem, rsem, to)
        cp.start()
        sends.append(cp)

    def arrived(dst, ssem, rsem):
        copy(dst, dst, ssem, rsem, dev(dc=1)).wait_recv()

    def piece(dy, dz, core=None):
        return ft.at[:, at_y(dy), at_z(dz), c if core is None else core]

    def to_sibling(dy, dz):
        send(piece(dy, dz), piece(dy, dz), c_s.at[dy, dz], c_r.at[dy, dz], dev(dc=1))

    def along_y(dz):
        for side, dy in ((0, 1), (1, 3)):
            send(piece(0, dz), piece(0, dz), y_s.at[side, dz], y_r.at[(-dy) % NY, dz], dev(dy=dy))

    def half(dy, dz, view):
        return ft.at[view, at_y(dy), at_z(dz), c]

    along_y(0)
    for dz in z_order:
        send(piece(0, 0), piece(0, 0), z_s.at[dz], z_r.at[(-dz) % NZ], dev(dz=dz))
    to_sibling(0, 0)

    def pass_on_y(dz):
        for side, dy in ((0, 3), (1, 1)):
            arrived(piece(dy, dz), y_s.at[0, 0], y_r.at[dy, dz])
            send(half(dy, dz, side), half(dy, dz, side), f_s.at[side, dz], f_r.at[side, dz], dev(dy=-dy))
            to_sibling(dy, dz)

    pass_on_y(0)
    for i, dz in enumerate(z_order):
        arrived(piece(0, dz), z_s.at[0], z_r.at[dz])
        along_y(dz)
        to_sibling(0, dz)
    for dz in z_order:
        pass_on_y(dz)
    for dz in [0] + z_order:
        for side in range(2):
            arrived(half(2, dz, side), f_s.at[0, 0], f_r.at[side, dz])
        to_sibling(2, dz)
    for dy in (0, 1, 3, 2):
        for dz in [0] + z_order:
            arrived(piece(dy, dz, 1 - c), c_s.at[0, 0], c_r.at[dy, dz])

    def row_square(i, acc):
        new = []
        for v in range(VIEWS):
            val = ft[v, lax.div(i, 16), lax.rem(lax.div(i, 2), 8), lax.rem(i, 2)].astype(F32)
            new.append(acc[v] + val * val)
        return tuple(new)

    acc = lax.fori_loop(0, D // PIECE, row_square, (jnp.zeros((16, RD), F32),) * 2)
    for v in range(VIEWS):
        rscale[v] = lax.rsqrt(jnp.sum(acc[v], axis=0, keepdims=True) + 1e-6)

    def lane_sum_row(tiles):
        return jnp.sum(tiles.T, axis=0, keepdims=True)

    tot[...] = jnp.zeros_like(tot)
    for v in range(VIEWS):
        def score_step(i, _, v=v):
            rows = pl.ds(pl.multiple_of(i * 128, 128), 128)
            raw = jnp.dot(ut[rows, :], ft[v].reshape(D, RD), preferred_element_type=F32)
            s = raw * rscale[v]
            sc[v, rows, :] = s
            e = jnp.exp2(s * EXP2_SCALE)
            k = e * e
            kn[v, rows, :] = k
            mass = k[:, 0:128]
            for j in range(1, RD // 128):
                mass = mass + k[:, j * 128:(j + 1) * 128]
            xbuf[0, 0, v, pl.ds(i, 1), :] = lane_sum_row(mass)
            for j in range(RD // 128):
                tot[v, j:j + 1, :] += jnp.sum(e[:, j * 128:(j + 1) * 128], axis=0, keepdims=True)
            return 0

        lax.fori_loop(0, KD // 128, score_step, 0)

    def column(buf, v, kb):
        return jnp.broadcast_to(buf[v, pl.ds(kb, 1), :], (128, 128)).T

    def sum_slots(buf, order):
        total = buf[order[0]]
        for i in order[1:]:
            total = total + buf[i]
        return total

    for t in range(ITERS):
        if t:
            for v in range(VIEWS):
                def mass_step(i, _, v=v):
                    rows = pl.ds(pl.multiple_of(i * 128, 128), 128)
                    mass = kn[v, rows, 0:128] * part[0, v, 0:1, :]
                    for j in range(1, RD // 128):
                        mass = mass + kn[v, rows, j * 128:(j + 1) * 128] * part[0, v, j:j + 1, :]
                    xbuf[t, 0, v, pl.ds(i, 1), :] = lane_sum_row(mass)
                    return 0

                lax.fori_loop(0, KD // 128, mass_step, 0)
        for dx in (1, 2, 3):
            send(xbuf.at[t, 0], xbuf.at[t, NX - dx], xs_s.at[t, dx], xs_r.at[t, NX - dx], dev(dx=dx))
        for dx in (1, 2, 3):
            arrived(xbuf.at[t, dx], xs_s.at[t, dx], xs_r.at[t, dx])
        part[1] = 1.0 / sum_slots(xbuf.at[t], range(NX))
        for v in range(VIEWS):
            def sample_step(i, acc, v=v):
                rows = pl.ds(pl.multiple_of(i * 128, 128), 128)
                col = column(part.at[1], v, i)
                return tuple(
                    acc[j] + jnp.sum((kn[v, rows, j * 128:(j + 1) * 128] * col).reshape(16, 8, 128), axis=0)
                    for j in range(RD // 128)
                )

            acc = lax.fori_loop(0, KD // 128, sample_step, (jnp.zeros((8, 128), F32),) * 8)
            for j in range(RD // 128):
                ybuf[t, 0, v, j:j + 1, :] = jnp.sum(acc[j], axis=0, keepdims=True)
        if t == 0:
            ybuf[t, 0, 2:4] = tot[...]
        n = 4 if t == 0 else 2
        for i, (dy, dc) in enumerate(yc_peers):
            j = yc_peers.index(((-dy) % NY, dc))
            send(ybuf.at[t, 0, 0:n], ybuf.at[t, 1 + j, 0:n], ys_s.at[t, i], ys_r.at[t, j], dev(dy=dy, dc=dc))
        for i in range(len(yc_peers)):
            arrived(ybuf.at[t, 1 + i, 0:n], ys_s.at[t, i], ys_r.at[t, i])
        zbuf[t, 0, 0:n] = sum_slots(ybuf.at[t, :, 0:n], range(8))
        for dz in z_order:
            send(zbuf.at[t, 0, 0:n], zbuf.at[t, NZ - dz, 0:n], zs_s.at[t, dz], zs_r.at[t, NZ - dz], dev(dz=dz))
        for dz in z_order:
            arrived(zbuf.at[t, dz, 0:n], zs_s.at[t, dz], zs_r.at[t, dz])
        sums = sum_slots(zbuf.at[t, :, 0:n], range(NZ))
        part[0] = 1.0 / sums[0:2]
        if t == 0:
            tot[...] = sums[2:4]

    factor, proto_factor = part.at[0], part.at[1]
    loss_acc = jnp.zeros((8, 128), F32)
    for v in range(VIEWS):
        loss_acc += jnp.log(tot[v]) * factor[1 - v] * ybuf[ITERS - 1, 0, 1 - v]
    loss_acc = -loss_acc

    def grad_block(dx, cols):
        out = None
        for v in range(VIEWS):
            lhs = ft[v, at_x(dx)].reshape(CHUNK, RD)
            d = lax.dot_general(lhs, sg[v, cols, :], NT, preferred_element_type=F32)
            out = d if out is None else out + d
        return out

    def weigh(dx, cols, delta):
        rows = pl.ds(pl.multiple_of(at_x(dx) * CHUNK, CHUNK), CHUNK)
        return jnp.sum(pv[rows, cols].astype(F32) * delta, axis=0, keepdims=True)

    for kc in range(CHUNKS):
        cols = slice(kc * CHUNK, (kc + 1) * CHUNK)

        def slope_step(i, acc, kc=kc):
            kb = kc * 2 + i
            rows = pl.ds(pl.multiple_of(kb * 128, 128), 128)
            for v in range(VIEWS):
                col = column(proto_factor, 1 - v, kb)
                for j in range(RD // 128):
                    lanes = slice(j * 128, (j + 1) * 128)
                    heated = rscale[v, :, lanes] * HEAT
                    s = sc[v, rows, lanes]
                    assign = kn[1 - v, rows, lanes] * col * factor[1 - v, j:j + 1, :]
                    pred = jnp.exp2(s * EXP2_SCALE) * (heated / tot[v, j:j + 1, :])
                    sg[v, rows, lanes] = (pred - assign * heated).astype(BF16)
                    acc = acc + jnp.sum((assign * s).reshape(16, 8, 128), axis=0) * HEAT
            return acc

        loss_acc = lax.fori_loop(0, 2, slope_step, loss_acc)
        delta = grad_block(2, cols)
        snd2[:, cols] = delta.astype(BF16)
        inner[0, :, cols] = weigh(2, cols, delta)
        send(snd2.at[0:128, cols], r1p.at[:, cols], h_s.at[0, kc], h_r.at[0, kc], dev(dx=1))
        send(snd2.at[128:256, cols], r1m.at[:, cols], h_s.at[1, kc], h_r.at[1, kc], dev(dx=3))

    ly[me_slot(y, c)] = loss_acc
    for i, (dy, dc) in enumerate(yc_peers):
        j = yc_peers.index(((-dy) % NY, dc))
        send(ly.at[me_slot(y, c)], ly.at[me_slot(y, c)], ly_s.at[i], ly_r.at[j], dev(dy=dy, dc=dc))

    for kc in range(CHUNKS):
        cols = slice(kc * CHUNK, (kc + 1) * CHUNK)
        dplus = grad_block(1, cols)
        dp[:, cols] = dplus
        sndp[128:256, cols] = dplus[128:256].astype(BF16)
        send(sndp.at[128:256, cols], recp.at[128:256, cols], d_s.at[0, kc], d_r.at[0, kc], dev(dx=1))
        dminus = grad_block(3, cols)
        dm[:, cols] = dminus
        sndm[0:128, cols] = dminus[0:128].astype(BF16)
        send(sndm.at[0:128, cols], recm.at[0:128, cols], d_s.at[1, kc], d_r.at[1, kc], dev(dx=3))
        own = grad_block(0, cols)
        down[:, cols] = own
        inner[0, :, cols] += weigh(1, cols, dplus) + weigh(3, cols, dminus) + weigh(0, cols, own)
    for dx in (1, 2, 3):
        send(inner.at[0], inner.at[NX - dx], in_s.at[dx], in_r.at[NX - dx], dev(dx=dx))

    for i, (dy, dc) in enumerate(yc_peers):
        slot = me_slot(at_y(dy), lax.rem(c + dc, NC))
        arrived(ly.at[slot], ly_s.at[i], ly_r.at[i])
    lz[z] = sum_slots(ly, range(8))
    for dz in z_order:
        send(lz.at[z], lz.at[z], lz_s.at[dz], lz_r.at[NZ - dz], dev(dz=dz))

    for kc in range(CHUNKS):
        cols = slice(kc * CHUNK, (kc + 1) * CHUNK)
        arrived(r1p.at[:, cols], h_s.at[0, kc], h_r.at[0, kc])
        sndp[0:128, cols] = (dp[0:128, cols] + r1p[:, cols].astype(F32)).astype(BF16)
        send(sndp.at[0:128, cols], recp.at[0:128, cols], e_s.at[0, kc], e_r.at[0, kc], dev(dx=1))
        arrived(r1m.at[:, cols], h_s.at[1, kc], h_r.at[1, kc])
        sndm[128:256, cols] = (dm[128:256, cols] + r1m[:, cols].astype(F32)).astype(BF16)
        send(sndm.at[128:256, cols], recm.at[128:256, cols], e_s.at[1, kc], e_r.at[1, kc], dev(dx=3))

    for dz in z_order:
        arrived(lz.at[at_z(dz)], lz_s.at[dz], lz_r.at[dz])
    lx[xi] = sum_slots(lz, range(NZ))
    for dx in (1, 2, 3):
        send(lx.at[xi], lx.at[xi], lx_s.at[dx], lx_r.at[NX - dx], dev(dx=dx))

    for dx in (1, 2, 3):
        arrived(inner.at[dx], in_s.at[dx], in_r.at[dx])
    weights = sum_slots(inner, range(NX)) * scale[...] * scale[...]
    own_rows = pl.ds(pl.multiple_of(xi * CHUNK, CHUNK), CHUNK)

    for dx in (1, 2, 3):
        arrived(lx.at[at_x(dx)], lx_s.at[dx], lx_r.at[dx])
    loss_ref[0, 0] = jnp.sum(sum_slots(lx, range(NX))) * (-1.0 / (2.0 * ROWS))

    for kc in range(CHUNKS):
        cols = slice(kc * CHUNK, (kc + 1) * CHUNK)
        arrived(recp.at[128:256, cols], d_s.at[0, kc], d_r.at[0, kc])
        arrived(recm.at[0:128, cols], d_s.at[1, kc], d_r.at[1, kc])
        arrived(recp.at[0:128, cols], e_s.at[0, kc], e_r.at[0, kc])
        arrived(recm.at[128:256, cols], e_s.at[1, kc], e_r.at[1, kc])
        delta = down[:, cols] + recp[:, cols].astype(F32) + recm[:, cols].astype(F32)
        grad_ref[:, cols] = scale[:, cols] * (delta - pv[own_rows, cols].astype(F32) * weights[:, cols])

    for cp in sends:
        cp.wait_send()


def me_slot(y, c):
    return y * NC + c


def per_device(features, prototypes):
    vmem = pltpu.VMEM
    dma = pltpu.SemaphoreType.DMA
    grad, loss = pl.pallas_call(
        kernel,
        out_shape=(jax.ShapeDtypeStruct((CHUNK, KD), F32), jax.ShapeDtypeStruct((1, 1), F32)),
        in_specs=[pl.BlockSpec(memory_space=pl.ANY)] * 2,
        out_specs=(pl.BlockSpec(memory_space=pltpu.VMEM), pl.BlockSpec(memory_space=pltpu.SMEM)),
        scratch_shapes=[
            vmem((VIEWS, NY, NZ, NC, PIECE, RD), BF16),
            vmem((D, KD), BF16),
            vmem((KD, D), BF16),
            vmem((VIEWS, KD, RD), F32),
            vmem((VIEWS, KD, RD), F32),
            vmem((VIEWS, KD, RD), BF16),
            vmem((1, KD), F32),
            vmem((VIEWS, 1, RD), F32),
            vmem((VIEWS, 8, 128), F32),
            vmem((2, VIEWS, 8, 128), F32),
            vmem((ITERS, NX, VIEWS, 8, 128), F32),
            vmem((ITERS, NY * NC, 4, 8, 128), F32),
            vmem((ITERS, NZ, 4, 8, 128), F32),
            vmem((NX, 8, 128), F32),
            vmem((NY * NC, 8, 128), F32),
            vmem((NZ, 8, 128), F32),
            vmem((NX, 1, KD), F32),
            vmem((CHUNK, KD), BF16),
            vmem((CHUNK, KD), BF16),
            vmem((CHUNK, KD), BF16),
            vmem((CHUNK // 2, KD), BF16),
            vmem((CHUNK // 2, KD), BF16),
            vmem((CHUNK, KD), BF16),
            vmem((CHUNK, KD), BF16),
            vmem((CHUNK, KD), F32),
            vmem((CHUNK, KD), F32),
            vmem((CHUNK, KD), F32),
            dma((2,)),
            dma((NZ,)), dma((NZ,)),
            dma((2, NZ)), dma((NY, NZ)),
            dma((2, NZ)), dma((2, NZ)),
            dma((NY, NZ)), dma((NY, NZ)),
            dma((ITERS, NX)), dma((ITERS, NX)),
            dma((ITERS, 7)), dma((ITERS, 7)),
            dma((ITERS, NZ)), dma((ITERS, NZ)),
            dma((NX,)), dma((NX,)),
            dma((7,)), dma((7,)),
            dma((NZ,)), dma((NZ,)),
            dma((NX,)), dma((NX,)),
            dma((2, CHUNKS)), dma((2, CHUNKS)),
            dma((2, CHUNKS)), dma((2, CHUNKS)),
            dma((2, CHUNKS)), dma((2, CHUNKS)),
        ],
        compiler_params=pltpu.CompilerParams(
            collective_id=0, has_side_effects=True, vmem_limit_bytes=56 * 2**20
        ),
    )(features.transpose(0, 2, 1), prototypes)
    return grad, loss[0, 0]


def solution(mesh):
    placed = (P(None, "batch", "proto"), P(None, "proto"))
    return jax.shard_map(
        per_device,
        mesh=mesh,
        in_specs=placed,
        out_specs=(P("batch", "proto"), P()),
        check_vma=False,
    )
```

```python
import functools
import math

import jax
import jax.numpy as jnp
from jax import lax
from jax.experimental import pallas as pl
from jax.experimental.pallas import tpu as pltpu
from jax.sharding import PartitionSpec as P

ITERS = 3
NX, NY, NZ, NC = 4, 4, 8, 2
VIEWS = 2
D = 1024
KD = 1024
RD = 1024
ROWS = NX * RD
PIECE = 16
CHUNK = 256
CHUNKS = KD // CHUNK
LANES = 256
BLOCKS = RD // LANES
HEAT = 10.0
EXP2_SCALE = 10.0 * math.log2(math.e)
F32 = jnp.float32
BF16 = jnp.bfloat16
NT = (((1,), (1,)), ((), ()))
EARLY, LATE = (0, 1, 7, 2), (6, 3, 5, 4)
GROUPS = (
    tuple((0, dz) for dz in EARLY + LATE),
    tuple((dy, dz) for dy in (1, 3) for dz in EARLY),
    tuple((dy, dz) for dy in (1, 3) for dz in LATE),
    tuple((2, dz) for dz in EARLY + LATE),
)


def kernel(feat_ref, proto_ref, grad_ref, loss_ref, ft, pv, ut, sc, kn, sg, scale, rscale, tot, part, xbuf, ybuf, zbuf,
           mass, lx, ly, lz, inner, snd2, sndp, sndm, r1p, r1m, recp, recm, dp, dm, down,
           in_sem, z_s, z_r, y_s, y_r, f_s, f_r, c_s, c_r, xs_s, xs_r, ys_s, ys_r, zs_s, zs_r,
           lx_s, lx_r, ly_s, ly_r, lz_s, lz_r, in_s, in_r, h_s, h_r, d_s, d_r, e_s, e_r):
    xi = lax.axis_index("batch")
    me = lax.axis_index("proto")
    c = lax.rem(me, NC)
    z = lax.rem(lax.div(me, NC), NZ)
    y = lax.div(me, NC * NZ)

    def at_y(dy):
        return lax.rem(y + dy % NY, NY)

    def at_z(dz):
        return lax.rem(z + dz % NZ, NZ)

    def at_x(dx):
        return lax.rem(xi + dx % NX, NX)

    def dev(dx=0, dy=0, dz=0, dc=0):
        return ((at_y(dy) * NZ + at_z(dz)) * NC + lax.rem(c + dc, NC), at_x(dx))

    yc_peers = [(dy, dc) for dy in (2, 1, 3, 0) for dc in range(NC) if dy or dc]
    z_order = [1, 7, 2, 6, 3, 5, 4]
    z_far = z_order[::-1]

    load_p = pltpu.make_async_copy(proto_ref, pv, in_sem.at[0])
    load_p.start()
    load_f = pltpu.make_async_copy(feat_ref, ft.at[:, y, z, c], in_sem.at[1])
    load_f.start()

    barrier = pltpu.get_barrier_semaphore()
    peers = [dev(dy=dy, dc=dc) for dy, dc in yc_peers]
    peers += [dev(dz=dz) for dz in z_order] + [dev(dx=dx) for dx in (1, 2, 3)]
    for peer in peers:
        pl.semaphore_signal(barrier, inc=1, device_id=peer, device_id_type=pl.DeviceIdType.MESH)

    load_p.wait()

    def square_step(i, acc):
        v = pv[pl.ds(pl.multiple_of(i * 16, 16), 16), :].astype(F32)
        return acc + v * v

    sq = lax.fori_loop(0, D // 16, square_step, jnp.zeros((16, KD), F32))
    scale[...] = lax.rsqrt(jnp.sum(sq, axis=0, keepdims=True) + 1e-6)

    def piece_rows(dy, dz):
        return pl.ds(pl.multiple_of((at_y(dy) * NZ + at_z(dz)) * 32, 32), 32)

    def unit_step(kb, _):
        cols = pl.ds(pl.multiple_of(kb * 128, 128), 128)
        for i in range(D // 128):
            four = [p for group in GROUPS for p in group][i * 4:i * 4 + 4]
            block = jnp.concatenate([pv[piece_rows(dy, dz), cols] for dy, dz in four], axis=0)
            ut[cols, i * 128:(i + 1) * 128] = (block.astype(F32) * scale[:, cols]).T.astype(BF16)
        return 0

    lax.fori_loop(0, KD // 128, unit_step, 0)
    load_f.wait()
    pl.semaphore_wait(barrier, len(peers))

    sends = []

    def copy(src, dst, ssem, rsem, to):
        return pltpu.make_async_remote_copy(
            src_ref=src, dst_ref=dst, send_sem=ssem, recv_sem=rsem, device_id=to, device_id_type=pl.DeviceIdType.MESH
        )

    def send(src, dst, ssem, rsem, to):
        cp = copy(src, dst, ssem, rsem, to)
        cp.start()
        sends.append(cp)

    def arrived(dst, ssem, rsem):
        copy(dst, dst, ssem, rsem, dev(dc=1)).wait_recv()

    def piece(dy, dz, core=None):
        return ft.at[:, at_y(dy), at_z(dz), c if core is None else core]

    def to_sibling(dy, dz):
        send(piece(dy, dz), piece(dy, dz), c_s.at[dy, dz], c_r.at[dy, dz], dev(dc=1))

    def from_sibling(g):
        for dy, dz in GROUPS[g]:
            arrived(piece(dy, dz, 1 - c), c_s.at[0, 0], c_r.at[dy, dz])

    def along_y(dz):
        for side, dy in ((0, 1), (1, 3)):
            send(piece(0, dz), piece(0, dz), y_s.at[side, dz], y_r.at[(-dy) % NY, dz], dev(dy=dy))

    def half(dy, dz, view):
        return ft.at[view, at_y(dy), at_z(dz), c]

    def pass_on_y(dz):
        for side, dy in ((0, 3), (1, 1)):
            arrived(piece(dy, dz), y_s.at[0, 0], y_r.at[dy, dz])
            send(half(dy, dz, side), half(dy, dz, side), f_s.at[side, dz], f_r.at[side, dz], dev(dy=-dy))
            to_sibling(dy, dz)

    def from_z(dz):
        arrived(piece(0, dz), z_s.at[0], z_r.at[dz])
        along_y(dz)
        to_sibling(0, dz)

    def opposite(dz):
        for side in range(2):
            arrived(half(2, dz, side), f_s.at[0, 0], f_r.at[side, dz])
        to_sibling(2, dz)

    def group_dot(g, v, bb):
        lanes = pl.ds(pl.multiple_of(bb * LANES, LANES), LANES)
        rhs = jnp.concatenate(
            [ft[v, at_y(dy), at_z(dz), :, :, lanes].reshape(NC * PIECE, LANES) for dy, dz in GROUPS[g]], axis=0
        )
        return lanes, jnp.dot(ut[:, g * CHUNK:(g + 1) * CHUNK], rhs, preferred_element_type=F32)

    def group_scores(g, v):
        def step(bb, _):
            lanes, d = group_dot(g, v, bb)
            if g == 0:
                sc[v, :, lanes] = d
            else:
                sc[v, :, lanes] += d
            return 0

        lax.fori_loop(0, BLOCKS, step, 0)

    def group_squares(g):
        def step(bb, _):
            lanes = pl.ds(pl.multiple_of(bb * 128, 128), 128)
            for v in range(VIEWS):
                total = jnp.zeros((PIECE, 128), F32)
                for dy, dz in GROUPS[g]:
                    for core in range(NC):
                        val = ft[v, at_y(dy), at_z(dz), core, :, lanes].astype(F32)
                        total = total + val * val
                total = jnp.sum(total, axis=0, keepdims=True)
                rscale[v, :, lanes] = total if g == 0 else rscale[v, :, lanes] + total
            return 0

        lax.fori_loop(0, RD // 128, step, 0)

    along_y(0)
    for dz in z_order:
        send(piece(0, 0), piece(0, 0), z_s.at[dz], z_r.at[(-dz) % NZ], dev(dz=dz))
    to_sibling(0, 0)
    from_z(1)
    from_z(7)
    pass_on_y(0)
    opposite(0)
    from_z(2)
    from_z(6)
    pass_on_y(1)
    pass_on_y(7)
    from_z(3)
    from_z(5)
    from_z(4)
    pass_on_y(2)
    opposite(1)
    from_sibling(0)
    group_scores(0, 0)
    pass_on_y(6)
    opposite(7)
    from_sibling(1)
    group_scores(0, 1)
    pass_on_y(3)
    group_scores(1, 0)
    pass_on_y(5)
    group_scores(1, 1)
    pass_on_y(4)
    group_squares(0)
    group_squares(1)
    opposite(2)
    opposite(6)
    from_sibling(2)
    group_scores(2, 0)
    opposite(3)
    opposite(5)
    group_scores(2, 1)
    opposite(4)
    group_squares(2)
    from_sibling(3)
    group_squares(3)
    for v in range(VIEWS):
        rscale[v] = lax.rsqrt(rscale[v] + 1e-6)

    def lane_sum_row(tiles):
        return jnp.sum(tiles.T, axis=0, keepdims=True)

    def column(buf, v, kb):
        return jnp.broadcast_to(buf[v, pl.ds(kb, 1), :], (128, 128)).T

    def sum_slots(buf, order):
        total = buf[order[0]]
        for i in order[1:]:
            total = total + buf[i]
        return total

    def last_scores(v):
        def step(bb, _):
            lanes, d = group_dot(3, v, bb)
            s = (sc[v, :, lanes] + d) * rscale[v, :, lanes]
            sc[v, :, lanes] = s
            e = jnp.exp2(s * EXP2_SCALE)
            k = e * e
            kn[v, :, lanes] = k
            mass[...] += k[:, 0:128] + k[:, 128:256]
            for j in range(LANES // 128):
                tot[v, pl.ds(bb * 2 + j, 1), :] = jnp.sum(e[:, j * 128:(j + 1) * 128], axis=0, keepdims=True)
            return 0

        mass[...] = jnp.zeros_like(mass)
        lax.fori_loop(0, BLOCKS, step, 0)
        for i in range(KD // 128):
            xbuf[0, v, 0, i:i + 1, :] = lane_sum_row(mass[i * 128:(i + 1) * 128, :])

    def proto_mass(t, v):
        def step(i, _):
            for kb in (i * 2, i * 2 + 1):
                rows = pl.ds(pl.multiple_of(kb * 128, 128), 128)
                total = kn[v, rows, 0:128] * part[0, v, 0:1, :]
                for j in range(1, RD // 128):
                    total = total + kn[v, rows, j * 128:(j + 1) * 128] * part[0, v, j:j + 1, :]
                xbuf[t, v, 0, pl.ds(kb, 1), :] = lane_sum_row(total)
            return 0

        lax.fori_loop(0, KD // 256, step, 0)

    def send_x(t, v):
        for dx in (2, 1, 3):
            send(xbuf.at[t, v, 0], xbuf.at[t, v, NX - dx], xs_s.at[t, v, dx], xs_r.at[t, v, NX - dx], dev(dx=dx))

    def sample_mass(t, v):
        for dx in (1, 3, 2):
            arrived(xbuf.at[t, v, dx], xs_s.at[t, v, dx], xs_r.at[t, v, dx])
        part[1, v] = 1.0 / sum_slots(xbuf.at[t, v], range(NX))

        def step(i, acc):
            for kb in (i * 2, i * 2 + 1):
                rows = pl.ds(pl.multiple_of(kb * 128, 128), 128)
                col = column(part.at[1], v, kb)
                acc = tuple(
                    acc[j] + jnp.sum((kn[v, rows, j * 128:(j + 1) * 128] * col).reshape(16, 8, 128), axis=0)
                    for j in range(RD // 128)
                )
            return acc

        acc = lax.fori_loop(0, KD // 256, step, (jnp.zeros((8, 128), F32),) * 8)
        for j in range(RD // 128):
            ybuf[t, v, 0, 0, j:j + 1, :] = jnp.sum(acc[j], axis=0, keepdims=True)
        if t == 0:
            ybuf[t, v, 0, 1] = tot[v]

    def send_y(t, v):
        n = 2 if t == 0 else 1
        for i, (dy, dc) in enumerate(yc_peers):
            j = yc_peers.index(((-dy) % NY, dc))
            send(ybuf.at[t, v, 0, 0:n], ybuf.at[t, v, 1 + j, 0:n], ys_s.at[t, v, i], ys_r.at[t, v, j], dev(dy=dy, dc=dc))

    def send_z(t, v):
        n = 2 if t == 0 else 1
        for i in range(len(yc_peers)):
            arrived(ybuf.at[t, v, 1 + i, 0:n], ys_s.at[t, v, i], ys_r.at[t, v, i])
        zbuf[t, v, 0, 0:n] = sum_slots(ybuf.at[t, v, :, 0:n], range(8))
        for dz in z_far:
            send(zbuf.at[t, v, 0, 0:n], zbuf.at[t, v, NZ - dz, 0:n], zs_s.at[t, v, dz], zs_r.at[t, v, NZ - dz], dev(dz=dz))

    def take_z(t, v):
        n = 2 if t == 0 else 1
        for dz in z_order:
            arrived(zbuf.at[t, v, dz, 0:n], zs_s.at[t, v, dz], zs_r.at[t, v, dz])
        sums = sum_slots(zbuf.at[t, v, :, 0:n], range(NZ))
        part[0, v] = 1.0 / sums[0]
        if t == 0:
            tot[v] = sums[1]

    for t in range(ITERS):
        for v in range(VIEWS):
            if t == 0:
                last_scores(v)
            else:
                take_z(t - 1, v)
                proto_mass(t, v)
            send_x(t, v)
        for v in range(VIEWS):
            sample_mass(t, v)
            send_y(t, v)
        for v in range(VIEWS):
            send_z(t, v)
    for v in range(VIEWS):
        take_z(ITERS - 1, v)

    factor, proto_factor = part.at[0], part.at[1]
    loss_acc = jnp.zeros((8, 128), F32)
    for v in range(VIEWS):
        loss_acc += jnp.log(tot[v]) * factor[1 - v] * ybuf[ITERS - 1, 1 - v, 0, 0]
    loss_acc = -loss_acc

    def grad_block(dx, cols):
        out = None
        for v in range(VIEWS):
            lhs = ft[v, at_x(dx)].reshape(CHUNK, RD)
            d = lax.dot_general(lhs, sg[v, cols, :], NT, preferred_element_type=F32)
            out = d if out is None else out + d
        return out

    def weigh(dx, cols, delta):
        rows = pl.ds(pl.multiple_of(at_x(dx) * CHUNK, CHUNK), CHUNK)
        return jnp.sum(pv[rows, cols].astype(F32) * delta, axis=0, keepdims=True)

    for kc in range(CHUNKS):
        cols = slice(kc * CHUNK, (kc + 1) * CHUNK)

        def slope_step(i, acc, kc=kc):
            kb = kc * 2 + i
            rows = pl.ds(pl.multiple_of(kb * 128, 128), 128)
            for v in range(VIEWS):
                col = column(proto_factor, 1 - v, kb)
                for j in range(RD // 128):
                    lanes = slice(j * 128, (j + 1) * 128)
                    heated = rscale[v, :, lanes] * HEAT
                    s = sc[v, rows, lanes]
                    assign = kn[1 - v, rows, lanes] * col * factor[1 - v, j:j + 1, :]
                    pred = jnp.exp2(s * EXP2_SCALE) * (heated / tot[v, j:j + 1, :])
                    sg[v, rows, lanes] = (pred - assign * heated).astype(BF16)
                    acc = acc + jnp.sum((assign * s).reshape(16, 8, 128), axis=0) * HEAT
            return acc

        loss_acc = lax.fori_loop(0, 2, slope_step, loss_acc)
        delta = grad_block(2, cols)
        snd2[:, cols] = delta.astype(BF16)
        inner[0, :, cols] = weigh(2, cols, delta)
        send(snd2.at[0:128, cols], r1p.at[:, cols], h_s.at[0, kc], h_r.at[0, kc], dev(dx=1))
        send(snd2.at[128:256, cols], r1m.at[:, cols], h_s.at[1, kc], h_r.at[1, kc], dev(dx=3))

    ly[me_slot(y, c)] = loss_acc
    for i, (dy, dc) in enumerate(yc_peers):
        j = yc_peers.index(((-dy) % NY, dc))
        send(ly.at[me_slot(y, c)], ly.at[me_slot(y, c)], ly_s.at[i], ly_r.at[j], dev(dy=dy, dc=dc))

    for kc in range(CHUNKS):
        cols = slice(kc * CHUNK, (kc + 1) * CHUNK)
        dplus = grad_block(1, cols)
        dp[:, cols] = dplus
        sndp[128:256, cols] = dplus[128:256].astype(BF16)
        send(sndp.at[128:256, cols], recp.at[128:256, cols], d_s.at[0, kc], d_r.at[0, kc], dev(dx=1))
        dminus = grad_block(3, cols)
        dm[:, cols] = dminus
        sndm[0:128, cols] = dminus[0:128].astype(BF16)
        send(sndm.at[0:128, cols], recm.at[0:128, cols], d_s.at[1, kc], d_r.at[1, kc], dev(dx=3))
        own = grad_block(0, cols)
        down[:, cols] = own
        inner[0, :, cols] += weigh(1, cols, dplus) + weigh(3, cols, dminus) + weigh(0, cols, own)
    for dx in (1, 2, 3):
        send(inner.at[0], inner.at[NX - dx], in_s.at[dx], in_r.at[NX - dx], dev(dx=dx))

    for i, (dy, dc) in enumerate(yc_peers):
        slot = me_slot(at_y(dy), lax.rem(c + dc, NC))
        arrived(ly.at[slot], ly_s.at[i], ly_r.at[i])
    lz[z] = sum_slots(ly, range(8))
    for dz in z_order:
        send(lz.at[z], lz.at[z], lz_s.at[dz], lz_r.at[NZ - dz], dev(dz=dz))

    for kc in range(CHUNKS):
        cols = slice(kc * CHUNK, (kc + 1) * CHUNK)
        arrived(r1p.at[:, cols], h_s.at[0, kc], h_r.at[0, kc])
        sndp[0:128, cols] = (dp[0:128, cols] + r1p[:, cols].astype(F32)).astype(BF16)
        send(sndp.at[0:128, cols], recp.at[0:128, cols], e_s.at[0, kc], e_r.at[0, kc], dev(dx=1))
        arrived(r1m.at[:, cols], h_s.at[1, kc], h_r.at[1, kc])
        sndm[128:256, cols] = (dm[128:256, cols] + r1m[:, cols].astype(F32)).astype(BF16)
        send(sndm.at[128:256, cols], recm.at[128:256, cols], e_s.at[1, kc], e_r.at[1, kc], dev(dx=3))

    for dz in z_order:
        arrived(lz.at[at_z(dz)], lz_s.at[dz], lz_r.at[dz])
    lx[xi] = sum_slots(lz, range(NZ))
    for dx in (1, 2, 3):
        send(lx.at[xi], lx.at[xi], lx_s.at[dx], lx_r.at[NX - dx], dev(dx=dx))

    for dx in (1, 2, 3):
        arrived(inner.at[dx], in_s.at[dx], in_r.at[dx])
    weights = sum_slots(inner, range(NX)) * scale[...] * scale[...]
    own_rows = pl.ds(pl.multiple_of(xi * CHUNK, CHUNK), CHUNK)

    for dx in (1, 2, 3):
        arrived(lx.at[at_x(dx)], lx_s.at[dx], lx_r.at[dx])
    loss_ref[0, 0] = jnp.sum(sum_slots(lx, range(NX))) * (-1.0 / (2.0 * ROWS))

    for kc in range(CHUNKS):
        cols = slice(kc * CHUNK, (kc + 1) * CHUNK)
        arrived(recp.at[128:256, cols], d_s.at[0, kc], d_r.at[0, kc])
        arrived(recm.at[0:128, cols], d_s.at[1, kc], d_r.at[1, kc])
        arrived(recp.at[0:128, cols], e_s.at[0, kc], e_r.at[0, kc])
        arrived(recm.at[128:256, cols], e_s.at[1, kc], e_r.at[1, kc])
        delta = down[:, cols] + recp[:, cols].astype(F32) + recm[:, cols].astype(F32)
        grad_ref[:, cols] = scale[:, cols] * (delta - pv[own_rows, cols].astype(F32) * weights[:, cols])

    for cp in sends:
        cp.wait_send()


def me_slot(y, c):
    return y * NC + c


def per_device(features, prototypes):
    vmem = pltpu.VMEM
    dma = pltpu.SemaphoreType.DMA
    grad, loss = pl.pallas_call(
        kernel,
        out_shape=(jax.ShapeDtypeStruct((CHUNK, KD), F32), jax.ShapeDtypeStruct((1, 1), F32)),
        in_specs=[pl.BlockSpec(memory_space=pl.ANY)] * 2,
        out_specs=(pl.BlockSpec(memory_space=pltpu.VMEM), pl.BlockSpec(memory_space=pltpu.SMEM)),
        scratch_shapes=[
            vmem((VIEWS, NY, NZ, NC, PIECE, RD), BF16),
            vmem((D, KD), BF16),
            vmem((KD, D), BF16),
            vmem((VIEWS, KD, RD), F32),
            vmem((VIEWS, KD, RD), F32),
            vmem((VIEWS, KD, RD), BF16),
            vmem((1, KD), F32),
            vmem((VIEWS, 1, RD), F32),
            vmem((VIEWS, 8, 128), F32),
            vmem((2, VIEWS, 8, 128), F32),
            vmem((ITERS, VIEWS, NX, 8, 128), F32),
            vmem((ITERS, VIEWS, NY * NC, 2, 8, 128), F32),
            vmem((ITERS, VIEWS, NZ, 2, 8, 128), F32),
            vmem((KD, 128), F32),
            vmem((NX, 8, 128), F32),
            vmem((NY * NC, 8, 128), F32),
            vmem((NZ, 8, 128), F32),
            vmem((NX, 1, KD), F32),
            vmem((CHUNK, KD), BF16),
            vmem((CHUNK, KD), BF16),
            vmem((CHUNK, KD), BF16),
            vmem((CHUNK // 2, KD), BF16),
            vmem((CHUNK // 2, KD), BF16),
            vmem((CHUNK, KD), BF16),
            vmem((CHUNK, KD), BF16),
            vmem((CHUNK, KD), F32),
            vmem((CHUNK, KD), F32),
            vmem((CHUNK, KD), F32),
            dma((2,)),
            dma((NZ,)), dma((NZ,)),
            dma((2, NZ)), dma((NY, NZ)),
            dma((2, NZ)), dma((2, NZ)),
            dma((NY, NZ)), dma((NY, NZ)),
            dma((ITERS, VIEWS, NX)), dma((ITERS, VIEWS, NX)),
            dma((ITERS, VIEWS, 7)), dma((ITERS, VIEWS, 7)),
            dma((ITERS, VIEWS, NZ)), dma((ITERS, VIEWS, NZ)),
            dma((NX,)), dma((NX,)),
            dma((7,)), dma((7,)),
            dma((NZ,)), dma((NZ,)),
            dma((NX,)), dma((NX,)),
            dma((2, CHUNKS)), dma((2, CHUNKS)),
            dma((2, CHUNKS)), dma((2, CHUNKS)),
            dma((2, CHUNKS)), dma((2, CHUNKS)),
        ],
        compiler_params=pltpu.CompilerParams(
            collective_id=0, has_side_effects=True, vmem_limit_bytes=56 * 2**20
        ),
    )(features.transpose(0, 2, 1), prototypes)
    return grad, loss[0, 0]


def solution(mesh):
    placed = (P(None, "batch", "proto"), P(None, "proto"))
    return jax.shard_map(
        per_device,
        mesh=mesh,
        in_specs=placed,
        out_specs=(P("batch", "proto"), P()),
        check_vma=False,
    )
```

```python
import functools
import math

import jax
import jax.numpy as jnp
from jax import lax
from jax.experimental import pallas as pl
from jax.experimental.pallas import tpu as pltpu
from jax.sharding import PartitionSpec as P

ITERS = 3
NX, NY, NZ, NC = 4, 4, 8, 2
VIEWS = 2
D = 1024
KD = 1024
RD = 1024
ROWS = NX * RD
PIECE = 16
CHUNK = 256
CHUNKS = KD // CHUNK
LANES = 256
BLOCKS = RD // LANES
HEAT = 10.0
EXP2_SCALE = 10.0 * math.log2(math.e)
F32 = jnp.float32
BF16 = jnp.bfloat16
NT = (((1,), (1,)), ((), ()))
Y_PLACES = (0, 1, 3, 2)
Z_PLACES = (0, 1, 7, 2, 6, 3, 5, 4)
STEPS = ((0, 1), (1, 3), (3, 5), (5, 7), (7, 8))
GROUPS = (((0, 1), (0, 8)), ((1, 3), (0, 4)), ((1, 3), (4, 8)), ((3, 4), (0, 8)))


def kernel(feat_ref, proto_ref, grad_ref, loss_ref, ft, pv, ut, sc, kn, sg, scale, rscale, tot, part, xbuf, ybuf, zbuf,
           mass, lx, ly, lz, inner, snd2, sndp, sndm, r1p, r1m, recp, recm, dp, dm, down,
           in_sem, z_s, z_r, y_s, y_r, f_s, f_r, c_s, c_r, xs_s, xs_r, ys_s, ys_r, zs_s, zs_r,
           lx_s, lx_r, ly_s, ly_r, lz_s, lz_r, in_s, in_r, h_s, h_r, d_s, d_r, e_s, e_r):
    xi = lax.axis_index("batch")
    me = lax.axis_index("proto")
    c = lax.rem(me, NC)
    z = lax.rem(lax.div(me, NC), NZ)
    y = lax.div(me, NC * NZ)

    def at_y(dy):
        return lax.rem(y + dy % NY, NY)

    def at_z(dz):
        return lax.rem(z + dz % NZ, NZ)

    def at_x(dx):
        return lax.rem(xi + dx % NX, NX)

    def dev(dx=0, dy=0, dz=0, dc=0):
        return ((at_y(dy) * NZ + at_z(dz)) * NC + lax.rem(c + dc, NC), at_x(dx))

    yc_peers = [(dy, dc) for dy in (2, 1, 3, 0) for dc in range(NC) if dy or dc]
    z_order = [1, 7, 2, 6, 3, 5, 4]
    z_far = z_order[::-1]

    load_p = pltpu.make_async_copy(proto_ref, pv, in_sem.at[0])
    load_p.start()
    load_f = pltpu.make_async_copy(feat_ref, ft.at[:, 0, 0, c], in_sem.at[1])
    load_f.start()

    barrier = pltpu.get_barrier_semaphore()
    peers = [dev(dy=dy, dc=dc) for dy, dc in yc_peers]
    peers += [dev(dz=dz) for dz in z_order] + [dev(dx=dx) for dx in (1, 2, 3)]
    for peer in peers:
        pl.semaphore_signal(barrier, inc=1, device_id=peer, device_id_type=pl.DeviceIdType.MESH)

    load_p.wait()

    def square_step(i, acc):
        v = pv[pl.ds(pl.multiple_of(i * 16, 16), 16), :].astype(F32)
        return acc + v * v

    sq = lax.fori_loop(0, D // 16, square_step, jnp.zeros((16, KD), F32))
    scale[...] = lax.rsqrt(jnp.sum(sq, axis=0, keepdims=True) + 1e-6)

    order = [
        (Y_PLACES[i], Z_PLACES[j]) for ys, zs in GROUPS for i in range(*ys) for j in range(*zs)
    ]

    def feature_rows(row_block, dz):
        return pl.ds(pl.multiple_of((row_block * NZ + at_z(dz)) * 32, 32), 32)

    def unit_step(kb, _):
        cols = pl.ds(pl.multiple_of(kb * 128, 128), 128)
        for i in range(D // 128):
            four = order[i * 4:i * 4 + 4]
            block = jnp.concatenate([pv[feature_rows(at_y(dy), dz), cols] for dy, dz in four], axis=0)
            ut[cols, i * 128:(i + 1) * 128] = (block.astype(F32) * scale[:, cols]).T.astype(BF16)
        return 0

    lax.fori_loop(0, KD // 128, unit_step, 0)
    load_f.wait()
    pl.semaphore_wait(barrier, len(peers))

    sends = []

    def copy(src, dst, ssem, rsem, to):
        return pltpu.make_async_remote_copy(
            src_ref=src, dst_ref=dst, send_sem=ssem, recv_sem=rsem, device_id=to, device_id_type=pl.DeviceIdType.MESH
        )

    def send(src, dst, ssem, rsem, to):
        cp = copy(src, dst, ssem, rsem, to)
        cp.start()
        sends.append(cp)

    def arrived(dst, ssem, rsem):
        copy(dst, dst, ssem, rsem, dev(dc=1)).wait_recv()

    def part_of(ys, zs, core=None):
        return ft.at[:, ys[0]:ys[1], zs[0]:zs[1], c if core is None else core]

    def to_sibling(kind, ys, q):
        send(part_of(ys, STEPS[q]), part_of(ys, STEPS[q]), c_s.at[kind, q], c_r.at[kind, q], dev(dc=1))

    def from_sibling(kind, steps):
        ys = ((0, 1), (1, 3), (3, 4))[kind]
        for q in steps:
            arrived(part_of(ys, STEPS[q], 1 - c), c_s.at[0, 0], c_r.at[kind, q])

    def along_y(q):
        for side, dy, place in ((0, 1, 2), (1, 3, 1)):
            send(part_of((0, 1), STEPS[q]), part_of((place, place + 1), STEPS[q]), y_s.at[side, q], y_r.at[side, q], dev(dy=dy))
        to_sibling(0, (0, 1), q)

    def half(place, q, view):
        return ft.at[view, place, STEPS[q][0]:STEPS[q][1], c]

    def pass_on_y(q):
        for side, dy, place in ((0, 1, 2), (1, 3, 1)):
            arrived(part_of((place, place + 1), STEPS[q]), y_s.at[0, 0], y_r.at[side, q])
            send(half(place, q, side), half(3, q, side), f_s.at[side, q], f_r.at[side, q], dev(dy=dy))
        to_sibling(1, (1, 3), q)

    def from_z(q):
        for j in range(*STEPS[q]):
            arrived(part_of((0, 1), (j, j + 1)), z_s.at[0], z_r.at[Z_PLACES[j]])
        along_y(q)

    def opposite(q):
        for side in range(2):
            arrived(half(3, q, side), f_s.at[0, 0], f_r.at[side, q])
        to_sibling(2, (3, 4), q)

    def group_dot(g, v, bb):
        lanes = pl.ds(pl.multiple_of(bb * LANES, LANES), LANES)
        ys, zs = GROUPS[g]
        rhs = ft[v, ys[0]:ys[1], zs[0]:zs[1], :, :, lanes].reshape(CHUNK, LANES)
        return lanes, jnp.dot(ut[:, g * CHUNK:(g + 1) * CHUNK], rhs, preferred_element_type=F32)

    def group_scores(g, v):
        def step(bb, _):
            lanes, d = group_dot(g, v, bb)
            if g == 0:
                sc[v, :, lanes] = d
            else:
                sc[v, :, lanes] += d
            return 0

        lax.fori_loop(0, BLOCKS, step, 0)

    def group_squares(g):
        def step(bb, _):
            lanes = pl.ds(pl.multiple_of(bb * 128, 128), 128)
            for v in range(VIEWS):
                ys, zs = GROUPS[g]
                val = ft[v, ys[0]:ys[1], zs[0]:zs[1], :, :, lanes].astype(F32)
                total = jnp.sum((val * val).reshape(CHUNK, 128), axis=0, keepdims=True)
                rscale[v, :, lanes] = total if g == 0 else rscale[v, :, lanes] + total
            return 0

        lax.fori_loop(0, RD // 128, step, 0)

    along_y(0)
    for dz in z_order:
        place = Z_PLACES.index(NZ - dz)
        send(part_of((0, 1), (0, 1)), part_of((0, 1), (place, place + 1)), z_s.at[dz], z_r.at[NZ - dz], dev(dz=dz))
    from_z(1)
    pass_on_y(0)
    opposite(0)
    from_z(2)
    pass_on_y(1)
    from_z(3)
    from_z(4)
    opposite(1)
    pass_on_y(2)
    from_sibling(0, range(5))
    group_scores(0, 0)
    group_scores(0, 1)
    pass_on_y(3)
    from_sibling(1, range(3))
    group_scores(1, 0)
    pass_on_y(4)
    group_scores(1, 1)
    opposite(2)
    group_squares(0)
    group_squares(1)
    from_sibling(1, range(3, 5))
    opposite(3)
    group_scores(2, 0)
    opposite(4)
    group_scores(2, 1)
    group_squares(2)
    from_sibling(2, range(5))
    group_squares(3)
    for v in range(VIEWS):
        rscale[v] = lax.rsqrt(rscale[v] + 1e-6)

    def lane_sum_row(tiles):
        return jnp.sum(tiles.T, axis=0, keepdims=True)

    def column(buf, v, kb):
        return jnp.broadcast_to(buf[v, pl.ds(kb, 1), :], (128, 128)).T

    def sum_slots(buf, order):
        total = buf[order[0]]
        for i in order[1:]:
            total = total + buf[i]
        return total

    def last_scores(v):
        def step(bb, _):
            lanes, d = group_dot(3, v, bb)
            s = (sc[v, :, lanes] + d) * rscale[v, :, lanes]
            sc[v, :, lanes] = s
            e = jnp.exp2(s * EXP2_SCALE)
            k = e * e
            kn[v, :, lanes] = k
            mass[...] += k[:, 0:128] + k[:, 128:256]
            for j in range(LANES // 128):
                tot[v, pl.ds(bb * 2 + j, 1), :] = jnp.sum(e[:, j * 128:(j + 1) * 128], axis=0, keepdims=True)
            return 0

        mass[...] = jnp.zeros_like(mass)
        lax.fori_loop(0, BLOCKS, step, 0)
        for i in range(KD // 128):
            xbuf[0, v, 0, i:i + 1, :] = lane_sum_row(mass[i * 128:(i + 1) * 128, :])

    def proto_mass(t, v):
        def step(i, _):
            for kb in (i * 2, i * 2 + 1):
                rows = pl.ds(pl.multiple_of(kb * 128, 128), 128)
                total = kn[v, rows, 0:128] * part[0, v, 0:1, :]
                for j in range(1, RD // 128):
                    total = total + kn[v, rows, j * 128:(j + 1) * 128] * part[0, v, j:j + 1, :]
                xbuf[t, v, 0, pl.ds(kb, 1), :] = lane_sum_row(total)
            return 0

        for i in range(KD // 256):
            step(i, 0)

    def send_x(t, v):
        for dx in (2, 1, 3):
            send(xbuf.at[t, v, 0], xbuf.at[t, v, NX - dx], xs_s.at[t, v, dx], xs_r.at[t, v, NX - dx], dev(dx=dx))

    def sample_mass(t, v):
        for dx in (1, 3, 2):
            arrived(xbuf.at[t, v, dx], xs_s.at[t, v, dx], xs_r.at[t, v, dx])
        part[1, v] = 1.0 / sum_slots(xbuf.at[t, v], range(NX))

        def step(i, acc):
            for kb in (i * 2, i * 2 + 1):
                rows = pl.ds(pl.multiple_of(kb * 128, 128), 128)
                col = column(part.at[1], v, kb)
                acc = tuple(
                    acc[j] + jnp.sum((kn[v, rows, j * 128:(j + 1) * 128] * col).reshape(16, 8, 128), axis=0)
                    for j in range(RD // 128)
                )
            return acc

        acc = (jnp.zeros((8, 128), F32),) * 8
        for i in range(KD // 256):
            acc = step(i, acc)
        for j in range(RD // 128):
            ybuf[t, v, 0, 0, j:j + 1, :] = jnp.sum(acc[j], axis=0, keepdims=True)
        if t == 0:
            ybuf[t, v, 0, 1] = tot[v]

    def send_y(t, v):
        n = 2 if t == 0 else 1
        for i, (dy, dc) in enumerate(yc_peers):
            j = yc_peers.index(((-dy) % NY, dc))
            send(ybuf.at[t, v, 0, 0:n], ybuf.at[t, v, 1 + j, 0:n], ys_s.at[t, v, i], ys_r.at[t, v, j], dev(dy=dy, dc=dc))

    def send_z(t, v):
        n = 2 if t == 0 else 1
        for i in range(len(yc_peers)):
            arrived(ybuf.at[t, v, 1 + i, 0:n], ys_s.at[t, v, i], ys_r.at[t, v, i])
        zbuf[t, v, 0, 0:n] = sum_slots(ybuf.at[t, v, :, 0:n], range(8))
        for dz in z_far:
            send(zbuf.at[t, v, 0, 0:n], zbuf.at[t, v, NZ - dz, 0:n], zs_s.at[t, v, dz], zs_r.at[t, v, NZ - dz], dev(dz=dz))

    def take_z(t, v):
        n = 2 if t == 0 else 1
        for dz in z_order:
            arrived(zbuf.at[t, v, dz, 0:n], zs_s.at[t, v, dz], zs_r.at[t, v, dz])
        sums = sum_slots(zbuf.at[t, v, :, 0:n], range(NZ))
        part[0, v] = 1.0 / sums[0]
        if t == 0:
            tot[v] = sums[1]

    for t in range(ITERS):
        for v in range(VIEWS):
            if t == 0:
                last_scores(v)
            else:
                take_z(t - 1, v)
                proto_mass(t, v)
            send_x(t, v)
        for v in range(VIEWS):
            sample_mass(t, v)
            send_y(t, v)
        for v in range(VIEWS):
            send_z(t, v)
    for v in range(VIEWS):
        take_z(ITERS - 1, v)

    factor, proto_factor = part.at[0], part.at[1]
    loss_acc = jnp.zeros((8, 128), F32)
    for v in range(VIEWS):
        loss_acc += jnp.log(tot[v]) * factor[1 - v] * ybuf[ITERS - 1, 1 - v, 0, 0]
    loss_acc = -loss_acc

    def y_place(row_block):
        dy = lax.rem(row_block + NY - y, NY)
        return dy + lax.div(dy, 2) * (5 - 2 * dy)

    def grad_block(dx, cols):
        out = None
        for v in range(VIEWS):
            lhs = ft[v, y_place(at_x(dx))].reshape(CHUNK, RD)
            d = lax.dot_general(lhs, sg[v, cols, :], NT, preferred_element_type=F32)
            out = d if out is None else out + d
        return out

    def weigh(dx, cols, delta):
        own = jnp.concatenate([pv[feature_rows(at_x(dx), dz), cols] for dz in Z_PLACES], axis=0)
        return jnp.sum(own.astype(F32) * delta, axis=0, keepdims=True)

    for kc in range(CHUNKS):
        cols = slice(kc * CHUNK, (kc + 1) * CHUNK)

        def slope_step(i, acc, kc=kc):
            kb = kc * 2 + i
            rows = pl.ds(pl.multiple_of(kb * 128, 128), 128)
            for v in range(VIEWS):
                col = column(proto_factor, 1 - v, kb)
                for j in range(RD // 128):
                    lanes = slice(j * 128, (j + 1) * 128)
                    heated = rscale[v, :, lanes] * HEAT
                    s = sc[v, rows, lanes]
                    assign = kn[1 - v, rows, lanes] * col * factor[1 - v, j:j + 1, :]
                    pred = jnp.exp2(s * EXP2_SCALE) * (heated / tot[v, j:j + 1, :])
                    sg[v, rows, lanes] = (pred - assign * heated).astype(BF16)
                    acc = acc + jnp.sum((assign * s).reshape(16, 8, 128), axis=0) * HEAT
            return acc

        loss_acc = lax.fori_loop(0, 2, slope_step, loss_acc)
        delta = grad_block(2, cols)
        snd2[:, cols] = delta.astype(BF16)
        inner[0, :, cols] = weigh(2, cols, delta)
        send(snd2.at[0:128, cols], r1p.at[:, cols], h_s.at[0, kc], h_r.at[0, kc], dev(dx=1))
        send(snd2.at[128:256, cols], r1m.at[:, cols], h_s.at[1, kc], h_r.at[1, kc], dev(dx=3))

    ly[me_slot(y, c)] = loss_acc
    for i, (dy, dc) in enumerate(yc_peers):
        j = yc_peers.index(((-dy) % NY, dc))
        send(ly.at[me_slot(y, c)], ly.at[me_slot(y, c)], ly_s.at[i], ly_r.at[j], dev(dy=dy, dc=dc))

    for kc in range(CHUNKS):
        cols = slice(kc * CHUNK, (kc + 1) * CHUNK)
        dplus = grad_block(1, cols)
        dp[:, cols] = dplus
        sndp[128:256, cols] = dplus[128:256].astype(BF16)
        send(sndp.at[128:256, cols], recp.at[128:256, cols], d_s.at[0, kc], d_r.at[0, kc], dev(dx=1))
        dminus = grad_block(3, cols)
        dm[:, cols] = dminus
        sndm[0:128, cols] = dminus[0:128].astype(BF16)
        send(sndm.at[0:128, cols], recm.at[0:128, cols], d_s.at[1, kc], d_r.at[1, kc], dev(dx=3))
        own = grad_block(0, cols)
        down[:, cols] = own
        inner[0, :, cols] += weigh(1, cols, dplus) + weigh(3, cols, dminus) + weigh(0, cols, own)
    for dx in (1, 2, 3):
        send(inner.at[0], inner.at[NX - dx], in_s.at[dx], in_r.at[NX - dx], dev(dx=dx))

    for i, (dy, dc) in enumerate(yc_peers):
        slot = me_slot(at_y(dy), lax.rem(c + dc, NC))
        arrived(ly.at[slot], ly_s.at[i], ly_r.at[i])
    lz[z] = sum_slots(ly, range(8))
    for dz in z_order:
        send(lz.at[z], lz.at[z], lz_s.at[dz], lz_r.at[NZ - dz], dev(dz=dz))

    for kc in range(CHUNKS):
        cols = slice(kc * CHUNK, (kc + 1) * CHUNK)
        arrived(r1p.at[:, cols], h_s.at[0, kc], h_r.at[0, kc])
        sndp[0:128, cols] = (dp[0:128, cols] + r1p[:, cols].astype(F32)).astype(BF16)
        send(sndp.at[0:128, cols], recp.at[0:128, cols], e_s.at[0, kc], e_r.at[0, kc], dev(dx=1))
        arrived(r1m.at[:, cols], h_s.at[1, kc], h_r.at[1, kc])
        sndm[128:256, cols] = (dm[128:256, cols] + r1m[:, cols].astype(F32)).astype(BF16)
        send(sndm.at[128:256, cols], recm.at[128:256, cols], e_s.at[1, kc], e_r.at[1, kc], dev(dx=3))

    for dz in z_order:
        arrived(lz.at[at_z(dz)], lz_s.at[dz], lz_r.at[dz])
    lx[xi] = sum_slots(lz, range(NZ))
    for dx in (1, 2, 3):
        send(lx.at[xi], lx.at[xi], lx_s.at[dx], lx_r.at[NX - dx], dev(dx=dx))

    for dx in (1, 2, 3):
        arrived(inner.at[dx], in_s.at[dx], in_r.at[dx])
    weights = sum_slots(inner, range(NX)) * scale[...] * scale[...]

    for dx in (1, 2, 3):
        arrived(lx.at[at_x(dx)], lx_s.at[dx], lx_r.at[dx])
    loss_ref[0, 0] = jnp.sum(sum_slots(lx, range(NX))) * (-1.0 / (2.0 * ROWS))

    for kc in range(CHUNKS):
        cols = slice(kc * CHUNK, (kc + 1) * CHUNK)
        arrived(recp.at[128:256, cols], d_s.at[0, kc], d_r.at[0, kc])
        arrived(recm.at[0:128, cols], d_s.at[1, kc], d_r.at[1, kc])
        arrived(recp.at[0:128, cols], e_s.at[0, kc], e_r.at[0, kc])
        arrived(recm.at[128:256, cols], e_s.at[1, kc], e_r.at[1, kc])
        delta = down[:, cols] + recp[:, cols].astype(F32) + recm[:, cols].astype(F32)
        for j, dz in enumerate(Z_PLACES):
            unit = pv[feature_rows(xi, dz), cols].astype(F32) * weights[:, cols]
            grad_ref[feature_rows(0, dz), cols] = scale[:, cols] * (delta[j * 32:(j + 1) * 32] - unit)

    for cp in sends:
        cp.wait_send()


def me_slot(y, c):
    return y * NC + c


def per_device(features, prototypes):
    vmem = pltpu.VMEM
    dma = pltpu.SemaphoreType.DMA
    grad, loss = pl.pallas_call(
        kernel,
        out_shape=(pltpu.VMEM((CHUNK, KD), F32), jax.ShapeDtypeStruct((1, 1), F32)),
        in_specs=[pl.BlockSpec(memory_space=pl.ANY)] * 2,
        out_specs=(pl.BlockSpec(memory_space=pltpu.VMEM), pl.BlockSpec(memory_space=pltpu.SMEM)),
        scratch_shapes=[
            vmem((VIEWS, NY, NZ, NC, PIECE, RD), BF16),
            vmem((D, KD), BF16),
            vmem((KD, D), BF16),
            vmem((VIEWS, KD, RD), F32),
            vmem((VIEWS, KD, RD), F32),
            vmem((VIEWS, KD, RD), BF16),
            vmem((1, KD), F32),
            vmem((VIEWS, 1, RD), F32),
            vmem((VIEWS, 8, 128), F32),
            vmem((2, VIEWS, 8, 128), F32),
            vmem((ITERS, VIEWS, NX, 8, 128), F32),
            vmem((ITERS, VIEWS, NY * NC, 2, 8, 128), F32),
            vmem((ITERS, VIEWS, NZ, 2, 8, 128), F32),
            vmem((KD, 128), F32),
            vmem((NX, 8, 128), F32),
            vmem((NY * NC, 8, 128), F32),
            vmem((NZ, 8, 128), F32),
            vmem((NX, 1, KD), F32),
            vmem((CHUNK, KD), BF16),
            vmem((CHUNK, KD), BF16),
            vmem((CHUNK, KD), BF16),
            vmem((CHUNK // 2, KD), BF16),
            vmem((CHUNK // 2, KD), BF16),
            vmem((CHUNK, KD), BF16),
            vmem((CHUNK, KD), BF16),
            vmem((CHUNK, KD), F32),
            vmem((CHUNK, KD), F32),
            vmem((CHUNK, KD), F32),
            dma((2,)),
            dma((NZ,)), dma((NZ,)),
            dma((2, 5)), dma((2, 5)),
            dma((2, 5)), dma((2, 5)),
            dma((3, 5)), dma((3, 5)),
            dma((ITERS, VIEWS, NX)), dma((ITERS, VIEWS, NX)),
            dma((ITERS, VIEWS, 7)), dma((ITERS, VIEWS, 7)),
            dma((ITERS, VIEWS, NZ)), dma((ITERS, VIEWS, NZ)),
            dma((NX,)), dma((NX,)),
            dma((7,)), dma((7,)),
            dma((NZ,)), dma((NZ,)),
            dma((NX,)), dma((NX,)),
            dma((2, CHUNKS)), dma((2, CHUNKS)),
            dma((2, CHUNKS)), dma((2, CHUNKS)),
            dma((2, CHUNKS)), dma((2, CHUNKS)),
        ],
        compiler_params=pltpu.CompilerParams(
            collective_id=0, has_side_effects=True, vmem_limit_bytes=56 * 2**20
        ),
    )(features.transpose(0, 2, 1), prototypes)
    return grad, loss[0, 0]


def solution(mesh):
    placed = (P(None, "batch", "proto"), P(None, "proto"))
    return jax.shard_map(
        per_device,
        mesh=mesh,
        in_specs=placed,
        out_specs=(P("batch", "proto"), P()),
        check_vma=False,
    )
```

```python
import functools
import math

import jax
import jax.numpy as jnp
from jax import lax
from jax.experimental import pallas as pl
from jax.experimental.pallas import tpu as pltpu
from jax.sharding import PartitionSpec as P

ITERS = 3
NX, NY, NZ, NC = 4, 4, 8, 2
VIEWS = 2
D = 1024
KD = 1024
RD = 1024
ROWS = NX * RD
PIECE = 16
CHUNK = 256
CHUNKS = KD // CHUNK
LANES = 256
BLOCKS = RD // LANES
HEAT = 10.0
EXP2_SCALE = 10.0 * math.log2(math.e)
F32 = jnp.float32
BF16 = jnp.bfloat16
NT = (((1,), (1,)), ((), ()))
Y_PLACES = (0, 1, 3, 2)
Z_PLACES = (0, 1, 7, 2, 6, 3, 5, 4)
STEPS = ((0, 1), (1, 3), (3, 5), (5, 7), (7, 8))
GROUPS = (((0, 1), (0, 8)), ((1, 3), (0, 4)), ((1, 3), (4, 8)), ((3, 4), (0, 8)))


def kernel(feat_ref, proto_ref, grad_ref, loss_ref, ft, pv, ut, sc, kn, sg, scale, rscale, tot, part, xbuf, ybuf, zbuf,
           mass, lx, ly, lz, inner, snd2, sndp, sndm, r1p, r1m, recp, recm, dp, dm, down,
           in_sem, z_s, z_r, y_s, y_r, f_s, f_r, c_s, c_r, xs_s, xs_r, ys_s, ys_r, zs_s, zs_r,
           lx_s, lx_r, ly_s, ly_r, lz_s, lz_r, in_s, in_r, h_s, h_r, d_s, d_r, e_s, e_r):
    xi = lax.axis_index("batch")
    me = lax.axis_index("proto")
    c = lax.rem(me, NC)
    z = lax.rem(lax.div(me, NC), NZ)
    y = lax.div(me, NC * NZ)

    def at_y(dy):
        return lax.rem(y + dy % NY, NY)

    def at_z(dz):
        return lax.rem(z + dz % NZ, NZ)

    def at_x(dx):
        return lax.rem(xi + dx % NX, NX)

    def dev(dx=0, dy=0, dz=0, dc=0):
        return ((at_y(dy) * NZ + at_z(dz)) * NC + lax.rem(c + dc, NC), at_x(dx))

    yc_peers = [(dy, dc) for dy in (2, 1, 3, 0) for dc in range(NC) if dy or dc]
    z_order = [1, 7, 2, 6, 3, 5, 4]
    z_far = z_order[::-1]

    load_p = pltpu.make_async_copy(proto_ref, pv, in_sem.at[0])
    load_p.start()
    load_f = pltpu.make_async_copy(feat_ref, ft.at[:, 0, 0, c], in_sem.at[1])
    load_f.start()

    barrier = pltpu.get_barrier_semaphore()
    peers = [dev(dy=dy, dc=dc) for dy, dc in yc_peers]
    peers += [dev(dz=dz) for dz in z_order] + [dev(dx=dx) for dx in (1, 2, 3)]
    for peer in peers:
        pl.semaphore_signal(barrier, inc=1, device_id=peer, device_id_type=pl.DeviceIdType.MESH)

    load_p.wait()

    def square_step(i, acc):
        v = pv[pl.ds(pl.multiple_of(i * 16, 16), 16), :].astype(F32)
        return acc + v * v

    sq = lax.fori_loop(0, D // 16, square_step, jnp.zeros((16, KD), F32))
    scale[...] = lax.rsqrt(jnp.sum(sq, axis=0, keepdims=True) + 1e-6)

    order = [
        (Y_PLACES[i], Z_PLACES[j]) for ys, zs in GROUPS for i in range(*ys) for j in range(*zs)
    ]

    def feature_rows(row_block, dz):
        return pl.ds(pl.multiple_of((row_block * NZ + at_z(dz)) * 32, 32), 32)

    def unit_step(kb, _):
        cols = pl.ds(pl.multiple_of(kb * 128, 128), 128)
        for i in range(D // 128):
            four = order[i * 4:i * 4 + 4]
            block = jnp.concatenate([pv[feature_rows(at_y(dy), dz), cols] for dy, dz in four], axis=0)
            ut[cols, i * 128:(i + 1) * 128] = (block.astype(F32) * scale[:, cols]).T.astype(BF16)
        return 0

    lax.fori_loop(0, KD // 128, unit_step, 0)
    load_f.wait()
    pl.semaphore_wait(barrier, len(peers))

    sends = []

    def copy(src, dst, ssem, rsem, to):
        return pltpu.make_async_remote_copy(
            src_ref=src, dst_ref=dst, send_sem=ssem, recv_sem=rsem, device_id=to, device_id_type=pl.DeviceIdType.MESH
        )

    def send(src, dst, ssem, rsem, to):
        cp = copy(src, dst, ssem, rsem, to)
        cp.start()
        sends.append(cp)

    def flush(count):
        for cp in sends[:count]:
            cp.wait_send()
        del sends[:count]

    def arrived(dst, ssem, rsem):
        copy(dst, dst, ssem, rsem, dev(dc=1)).wait_recv()

    def part_of(ys, zs, core=None):
        return ft.at[:, ys[0]:ys[1], zs[0]:zs[1], c if core is None else core]

    def to_sibling(kind, ys, q):
        send(part_of(ys, STEPS[q]), part_of(ys, STEPS[q]), c_s.at[kind, q], c_r.at[kind, q], dev(dc=1))

    def from_sibling(kind, steps):
        ys = ((0, 1), (1, 3), (3, 4))[kind]
        for q in steps:
            arrived(part_of(ys, STEPS[q], 1 - c), c_s.at[0, 0], c_r.at[kind, q])

    def along_y(q):
        for side, dy, place in ((0, 1, 2), (1, 3, 1)):
            send(part_of((0, 1), STEPS[q]), part_of((place, place + 1), STEPS[q]), y_s.at[side, q], y_r.at[side, q], dev(dy=dy))
        to_sibling(0, (0, 1), q)

    def half(place, q, view):
        return ft.at[view, place, STEPS[q][0]:STEPS[q][1], c]

    def pass_on_y(q):
        for side, dy, place in ((0, 1, 2), (1, 3, 1)):
            arrived(part_of((place, place + 1), STEPS[q]), y_s.at[0, 0], y_r.at[side, q])
            send(half(place, q, side), half(3, q, side), f_s.at[side, q], f_r.at[side, q], dev(dy=dy))
        to_sibling(1, (1, 3), q)

    def from_z(q):
        for j in range(*STEPS[q]):
            arrived(part_of((0, 1), (j, j + 1)), z_s.at[0], z_r.at[Z_PLACES[j]])
        along_y(q)

    def opposite(q):
        for side in range(2):
            arrived(half(3, q, side), f_s.at[0, 0], f_r.at[side, q])
        to_sibling(2, (3, 4), q)

    def group_dot(g, v, bb):
        lanes = pl.ds(pl.multiple_of(bb * LANES, LANES), LANES)
        ys, zs = GROUPS[g]
        rhs = ft[v, ys[0]:ys[1], zs[0]:zs[1], :, :, lanes].reshape(CHUNK, LANES)
        return lanes, jnp.dot(ut[:, g * CHUNK:(g + 1) * CHUNK], rhs, preferred_element_type=F32)

    def group_scores(g, v):
        def step(bb, _):
            lanes, d = group_dot(g, v, bb)
            if g == 0:
                sc[v, :, lanes] = d
            else:
                sc[v, :, lanes] += d
            return 0

        lax.fori_loop(0, BLOCKS, step, 0)

    def group_squares(g):
        def step(bb, _):
            lanes = pl.ds(pl.multiple_of(bb * 128, 128), 128)
            for v in range(VIEWS):
                ys, zs = GROUPS[g]
                val = ft[v, ys[0]:ys[1], zs[0]:zs[1], :, :, lanes].astype(F32)
                total = jnp.sum((val * val).reshape(CHUNK, 128), axis=0, keepdims=True)
                rscale[v, :, lanes] = total if g == 0 else rscale[v, :, lanes] + total
            return 0

        lax.fori_loop(0, RD // 128, step, 0)

    along_y(0)
    for dz in z_order:
        place = Z_PLACES.index(NZ - dz)
        send(part_of((0, 1), (0, 1)), part_of((0, 1), (place, place + 1)), z_s.at[dz], z_r.at[NZ - dz], dev(dz=dz))
    from_z(1)
    pass_on_y(0)
    opposite(0)
    from_z(2)
    pass_on_y(1)
    from_z(3)
    from_z(4)
    opposite(1)
    pass_on_y(2)
    from_sibling(0, range(5))
    group_scores(0, 0)
    group_scores(0, 1)
    pass_on_y(3)
    from_sibling(1, range(3))
    group_scores(1, 0)
    pass_on_y(4)
    group_scores(1, 1)
    opposite(2)
    group_squares(0)
    group_squares(1)
    from_sibling(1, range(3, 5))
    opposite(3)
    group_scores(2, 0)
    opposite(4)
    group_scores(2, 1)
    group_squares(2)
    from_sibling(2, range(5))
    group_squares(3)
    for v in range(VIEWS):
        rscale[v] = lax.rsqrt(rscale[v] + 1e-6)

    def lane_sum_row(tiles):
        return jnp.sum(tiles.T, axis=0, keepdims=True)

    def column(buf, v, kb):
        return jnp.broadcast_to(buf[v, pl.ds(kb, 1), :], (128, 128)).T

    def sum_slots(buf, order):
        total = buf[order[0]]
        for i in order[1:]:
            total = total + buf[i]
        return total

    def last_scores(v):
        def step(bb, _):
            lanes, d = group_dot(3, v, bb)
            s = (sc[v, :, lanes] + d) * rscale[v, :, lanes]
            sc[v, :, lanes] = s
            e = jnp.exp2(s * EXP2_SCALE)
            k = e * e
            kn[v, :, lanes] = k
            mass[...] += k[:, 0:128] + k[:, 128:256]
            for j in range(LANES // 128):
                tot[v, pl.ds(bb * 2 + j, 1), :] = jnp.sum(e[:, j * 128:(j + 1) * 128], axis=0, keepdims=True)
            return 0

        mass[...] = jnp.zeros_like(mass)
        for bb in range(BLOCKS):
            step(bb, 0)
        for i in range(KD // 128):
            xbuf[0, v, 0, i:i + 1, :] = lane_sum_row(mass[i * 128:(i + 1) * 128, :])

    def proto_mass(t, v):
        def step(i, _):
            for kb in (i * 2, i * 2 + 1):
                rows = pl.ds(pl.multiple_of(kb * 128, 128), 128)
                total = kn[v, rows, 0:128] * part[0, v, 0:1, :]
                for j in range(1, RD // 128):
                    total = total + kn[v, rows, j * 128:(j + 1) * 128] * part[0, v, j:j + 1, :]
                xbuf[t, v, 0, pl.ds(kb, 1), :] = lane_sum_row(total)
            return 0

        for i in range(KD // 256):
            step(i, 0)

    def send_x(t, v):
        for dx in (2, 1, 3):
            send(xbuf.at[t, v, 0], xbuf.at[t, v, NX - dx], xs_s.at[t, v, dx], xs_r.at[t, v, NX - dx], dev(dx=dx))

    def sample_mass(t, v):
        for dx in (1, 3, 2):
            arrived(xbuf.at[t, v, dx], xs_s.at[t, v, dx], xs_r.at[t, v, dx])
        part[1, v] = 1.0 / sum_slots(xbuf.at[t, v], range(NX))

        def step(i, acc):
            for kb in (i * 2, i * 2 + 1):
                rows = pl.ds(pl.multiple_of(kb * 128, 128), 128)
                col = column(part.at[1], v, kb)
                acc = tuple(
                    acc[j] + jnp.sum((kn[v, rows, j * 128:(j + 1) * 128] * col).reshape(16, 8, 128), axis=0)
                    for j in range(RD // 128)
                )
            return acc

        acc = (jnp.zeros((8, 128), F32),) * 8
        for i in range(KD // 256):
            acc = step(i, acc)
        for j in range(RD // 128):
            ybuf[t, v, 0, 0, j:j + 1, :] = jnp.sum(acc[j], axis=0, keepdims=True)
        if t == 0:
            ybuf[t, v, 0, 1] = tot[v]

    def send_y(t, v):
        n = 2 if t == 0 else 1
        for i, (dy, dc) in enumerate(yc_peers):
            j = yc_peers.index(((-dy) % NY, dc))
            send(ybuf.at[t, v, 0, 0:n], ybuf.at[t, v, 1 + j, 0:n], ys_s.at[t, v, i], ys_r.at[t, v, j], dev(dy=dy, dc=dc))

    def send_z(t, v):
        n = 2 if t == 0 else 1
        for i in range(len(yc_peers)):
            arrived(ybuf.at[t, v, 1 + i, 0:n], ys_s.at[t, v, i], ys_r.at[t, v, i])
        zbuf[t, v, 0, 0:n] = sum_slots(ybuf.at[t, v, :, 0:n], range(8))
        for dz in z_far:
            send(zbuf.at[t, v, 0, 0:n], zbuf.at[t, v, NZ - dz, 0:n], zs_s.at[t, v, dz], zs_r.at[t, v, NZ - dz], dev(dz=dz))

    def take_z(t, v):
        n = 2 if t == 0 else 1
        for dz in z_order:
            arrived(zbuf.at[t, v, dz, 0:n], zs_s.at[t, v, dz], zs_r.at[t, v, dz])
        sums = sum_slots(zbuf.at[t, v, :, 0:n], range(NZ))
        part[0, v] = 1.0 / sums[0]
        if t == 0:
            tot[v] = sums[1]

    for t in range(ITERS):
        older = len(sends)
        for v in range(VIEWS):
            if t == 0:
                last_scores(v)
            else:
                take_z(t - 1, v)
                proto_mass(t, v)
            send_x(t, v)
        flush(older)
        for v in range(VIEWS):
            sample_mass(t, v)
            send_y(t, v)
        for v in range(VIEWS):
            send_z(t, v)
    for v in range(VIEWS):
        take_z(ITERS - 1, v)

    older = len(sends)

    factor, proto_factor = part.at[0], part.at[1]
    loss_acc = jnp.zeros((8, 128), F32)
    for v in range(VIEWS):
        loss_acc += jnp.log(tot[v]) * factor[1 - v] * ybuf[ITERS - 1, 1 - v, 0, 0]
    loss_acc = -loss_acc

    def y_place(row_block):
        dy = lax.rem(row_block + NY - y, NY)
        return dy + lax.div(dy, 2) * (5 - 2 * dy)

    def grad_block(dx, cols):
        out = None
        for v in range(VIEWS):
            lhs = ft[v, y_place(at_x(dx))].reshape(CHUNK, RD)
            d = lax.dot_general(lhs, sg[v, cols, :], NT, preferred_element_type=F32)
            out = d if out is None else out + d
        return out

    def weigh(dx, cols, delta):
        own = jnp.concatenate([pv[feature_rows(at_x(dx), dz), cols] for dz in Z_PLACES], axis=0)
        return jnp.sum(own.astype(F32) * delta, axis=0, keepdims=True)

    for kc in range(CHUNKS):
        cols = slice(kc * CHUNK, (kc + 1) * CHUNK)

        def slope_step(i, acc, kc=kc):
            kb = kc * 2 + i
            rows = pl.ds(pl.multiple_of(kb * 128, 128), 128)
            for v in range(VIEWS):
                col = column(proto_factor, 1 - v, kb)
                for j in range(RD // 128):
                    lanes = slice(j * 128, (j + 1) * 128)
                    heated = rscale[v, :, lanes] * HEAT
                    s = sc[v, rows, lanes]
                    assign = kn[1 - v, rows, lanes] * col * factor[1 - v, j:j + 1, :]
                    pred = jnp.exp2(s * EXP2_SCALE) * (heated / tot[v, j:j + 1, :])
                    sg[v, rows, lanes] = (pred - assign * heated).astype(BF16)
                    acc = acc + jnp.sum((assign * s).reshape(16, 8, 128), axis=0) * HEAT
            return acc

        loss_acc = slope_step(1, slope_step(0, loss_acc))
        delta = grad_block(2, cols)
        snd2[:, cols] = delta.astype(BF16)
        inner[0, :, cols] = weigh(2, cols, delta)
        send(snd2.at[0:128, cols], r1p.at[:, cols], h_s.at[0, kc], h_r.at[0, kc], dev(dx=1))
        send(snd2.at[128:256, cols], r1m.at[:, cols], h_s.at[1, kc], h_r.at[1, kc], dev(dx=3))

    ly[me_slot(y, c)] = loss_acc
    for i, (dy, dc) in enumerate(yc_peers):
        j = yc_peers.index(((-dy) % NY, dc))
        send(ly.at[me_slot(y, c)], ly.at[me_slot(y, c)], ly_s.at[i], ly_r.at[j], dev(dy=dy, dc=dc))

    for kc in range(CHUNKS):
        cols = slice(kc * CHUNK, (kc + 1) * CHUNK)
        dplus = grad_block(1, cols)
        dp[:, cols] = dplus
        sndp[128:256, cols] = dplus[128:256].astype(BF16)
        send(sndp.at[128:256, cols], recp.at[128:256, cols], d_s.at[0, kc], d_r.at[0, kc], dev(dx=1))
        dminus = grad_block(3, cols)
        dm[:, cols] = dminus
        sndm[0:128, cols] = dminus[0:128].astype(BF16)
        send(sndm.at[0:128, cols], recm.at[0:128, cols], d_s.at[1, kc], d_r.at[1, kc], dev(dx=3))
        own = grad_block(0, cols)
        down[:, cols] = own
        inner[0, :, cols] += weigh(1, cols, dplus) + weigh(3, cols, dminus) + weigh(0, cols, own)
    flush(older)
    older = len(sends)
    for dx in (1, 2, 3):
        send(inner.at[0], inner.at[NX - dx], in_s.at[dx], in_r.at[NX - dx], dev(dx=dx))

    for i, (dy, dc) in enumerate(yc_peers):
        slot = me_slot(at_y(dy), lax.rem(c + dc, NC))
        arrived(ly.at[slot], ly_s.at[i], ly_r.at[i])
    lz[z] = sum_slots(ly, range(8))
    for dz in z_order:
        send(lz.at[z], lz.at[z], lz_s.at[dz], lz_r.at[NZ - dz], dev(dz=dz))

    for kc in range(CHUNKS):
        cols = slice(kc * CHUNK, (kc + 1) * CHUNK)
        arrived(r1p.at[:, cols], h_s.at[0, kc], h_r.at[0, kc])
        sndp[0:128, cols] = (dp[0:128, cols] + r1p[:, cols].astype(F32)).astype(BF16)
        send(sndp.at[0:128, cols], recp.at[0:128, cols], e_s.at[0, kc], e_r.at[0, kc], dev(dx=1))
        arrived(r1m.at[:, cols], h_s.at[1, kc], h_r.at[1, kc])
        sndm[128:256, cols] = (dm[128:256, cols] + r1m[:, cols].astype(F32)).astype(BF16)
        send(sndm.at[128:256, cols], recm.at[128:256, cols], e_s.at[1, kc], e_r.at[1, kc], dev(dx=3))

    flush(older)
    older = len(sends)
    for dz in z_order:
        arrived(lz.at[at_z(dz)], lz_s.at[dz], lz_r.at[dz])
    lx[xi] = sum_slots(lz, range(NZ))
    for dx in (1, 2, 3):
        send(lx.at[xi], lx.at[xi], lx_s.at[dx], lx_r.at[NX - dx], dev(dx=dx))

    for dx in (1, 2, 3):
        arrived(inner.at[dx], in_s.at[dx], in_r.at[dx])
    weights = sum_slots(inner, range(NX)) * scale[...] * scale[...]

    for kc in range(CHUNKS):
        cols = slice(kc * CHUNK, (kc + 1) * CHUNK)
        arrived(recp.at[128:256, cols], d_s.at[0, kc], d_r.at[0, kc])
        arrived(recm.at[0:128, cols], d_s.at[1, kc], d_r.at[1, kc])
        arrived(recp.at[0:128, cols], e_s.at[0, kc], e_r.at[0, kc])
        arrived(recm.at[128:256, cols], e_s.at[1, kc], e_r.at[1, kc])
        delta = down[:, cols] + recp[:, cols].astype(F32) + recm[:, cols].astype(F32)
        for j, dz in enumerate(Z_PLACES):
            unit = pv[feature_rows(xi, dz), cols].astype(F32) * weights[:, cols]
            grad_ref[feature_rows(0, dz), cols] = scale[:, cols] * (delta[j * 32:(j + 1) * 32] - unit)

    flush(older)
    for dx in (1, 2, 3):
        arrived(lx.at[at_x(dx)], lx_s.at[dx], lx_r.at[dx])
    loss_ref[0, 0] = jnp.sum(sum_slots(lx, range(NX))) * (-1.0 / (2.0 * ROWS))

    flush(len(sends))


def me_slot(y, c):
    return y * NC + c


def per_device(features, prototypes):
    vmem = pltpu.VMEM
    dma = pltpu.SemaphoreType.DMA
    grad, loss = pl.pallas_call(
        kernel,
        out_shape=(pltpu.VMEM((CHUNK, KD), F32), jax.ShapeDtypeStruct((1, 1), F32)),
        in_specs=[pl.BlockSpec(memory_space=pl.ANY)] * 2,
        out_specs=(pl.BlockSpec(memory_space=pltpu.VMEM), pl.BlockSpec(memory_space=pltpu.SMEM)),
        scratch_shapes=[
            vmem((VIEWS, NY, NZ, NC, PIECE, RD), BF16),
            vmem((D, KD), BF16),
            vmem((KD, D), BF16),
            vmem((VIEWS, KD, RD), F32),
            vmem((VIEWS, KD, RD), F32),
            vmem((VIEWS, KD, RD), BF16),
            vmem((1, KD), F32),
            vmem((VIEWS, 1, RD), F32),
            vmem((VIEWS, 8, 128), F32),
            vmem((2, VIEWS, 8, 128), F32),
            vmem((ITERS, VIEWS, NX, 8, 128), F32),
            vmem((ITERS, VIEWS, NY * NC, 2, 8, 128), F32),
            vmem((ITERS, VIEWS, NZ, 2, 8, 128), F32),
            vmem((KD, 128), F32),
            vmem((NX, 8, 128), F32),
            vmem((NY * NC, 8, 128), F32),
            vmem((NZ, 8, 128), F32),
            vmem((NX, 1, KD), F32),
            vmem((CHUNK, KD), BF16),
            vmem((CHUNK, KD), BF16),
            vmem((CHUNK, KD), BF16),
            vmem((CHUNK // 2, KD), BF16),
            vmem((CHUNK // 2, KD), BF16),
            vmem((CHUNK, KD), BF16),
            vmem((CHUNK, KD), BF16),
            vmem((CHUNK, KD), F32),
            vmem((CHUNK, KD), F32),
            vmem((CHUNK, KD), F32),
            dma((2,)),
            dma((NZ,)), dma((NZ,)),
            dma((2, 5)), dma((2, 5)),
            dma((2, 5)), dma((2, 5)),
            dma((3, 5)), dma((3, 5)),
            dma((ITERS, VIEWS, NX)), dma((ITERS, VIEWS, NX)),
            dma((ITERS, VIEWS, 7)), dma((ITERS, VIEWS, 7)),
            dma((ITERS, VIEWS, NZ)), dma((ITERS, VIEWS, NZ)),
            dma((NX,)), dma((NX,)),
            dma((7,)), dma((7,)),
            dma((NZ,)), dma((NZ,)),
            dma((NX,)), dma((NX,)),
            dma((2, CHUNKS)), dma((2, CHUNKS)),
            dma((2, CHUNKS)), dma((2, CHUNKS)),
            dma((2, CHUNKS)), dma((2, CHUNKS)),
        ],
        compiler_params=pltpu.CompilerParams(
            collective_id=0, has_side_effects=True, vmem_limit_bytes=56 * 2**20
        ),
    )(features.transpose(0, 2, 1), prototypes)
    return grad, loss[0, 0]


def solution(mesh):
    placed = (P(None, "batch", "proto"), P(None, "proto"))
    return jax.shard_map(
        per_device,
        mesh=mesh,
        in_specs=placed,
        out_specs=(P("batch", "proto"), P()),
        check_vma=False,
    )
```

```python
import functools
import math

import jax
import jax.numpy as jnp
from jax import lax
from jax.experimental import pallas as pl
from jax.experimental.pallas import tpu as pltpu
from jax.sharding import PartitionSpec as P

ITERS = 3
NX, NY, NZ, NC = 4, 4, 8, 2
VIEWS = 2
D = 1024
KD = 1024
RD = 1024
ROWS = NX * RD
PIECE = 16
CHUNK = 256
CHUNKS = KD // CHUNK
LANES = 256
BLOCKS = RD // LANES
HEAT = 10.0
EXP2_SCALE = 10.0 * math.log2(math.e)
F32 = jnp.float32
BF16 = jnp.bfloat16
NT = (((1,), (1,)), ((), ()))
Y_PLACES = (0, 1, 3, 2)
Z_PLACES = (0, 1, 7, 2, 6, 3, 5, 4)
STEPS = ((0, 1), (1, 3), (3, 5), (5, 7), (7, 8))
GROUPS = (((0, 1), (0, 8)), ((1, 3), (0, 4)), ((1, 3), (4, 8)), ((3, 4), (0, 8)))


def kernel(feat_ref, proto_ref, grad_ref, loss_ref, ft, pv, ut, sc, kn, pred, sg, scale, rscale, tot, part, xbuf, ybuf, zbuf,
           mass, lx, ly, lz, inner, snd2, sndp, sndm, r1p, r1m, recp, recm, dp, dm, down,
           in_sem, z_s, z_r, y_s, y_r, f_s, f_r, c_s, c_r, xs_s, xs_r, ys_s, ys_r, zs_s, zs_r,
           lx_s, lx_r, ly_s, ly_r, lz_s, lz_r, in_s, in_r, h_s, h_r, d_s, d_r, e_s, e_r):
    xi = lax.axis_index("batch")
    me = lax.axis_index("proto")
    c = lax.rem(me, NC)
    z = lax.rem(lax.div(me, NC), NZ)
    y = lax.div(me, NC * NZ)

    def at_y(dy):
        return lax.rem(y + dy % NY, NY)

    def at_z(dz):
        return lax.rem(z + dz % NZ, NZ)

    def at_x(dx):
        return lax.rem(xi + dx % NX, NX)

    def dev(dx=0, dy=0, dz=0, dc=0):
        return ((at_y(dy) * NZ + at_z(dz)) * NC + lax.rem(c + dc, NC), at_x(dx))

    yc_peers = [(dy, dc) for dy in (2, 1, 3, 0) for dc in range(NC) if dy or dc]
    z_order = [1, 7, 2, 6, 3, 5, 4]
    z_far = z_order[::-1]

    load_p = pltpu.make_async_copy(proto_ref, pv, in_sem.at[0])
    load_p.start()
    load_f = pltpu.make_async_copy(feat_ref, ft.at[:, 0, 0, c], in_sem.at[1])
    load_f.start()

    barrier = pltpu.get_barrier_semaphore()
    peers = [dev(dy=dy, dc=dc) for dy, dc in yc_peers]
    peers += [dev(dz=dz) for dz in z_order] + [dev(dx=dx) for dx in (1, 2, 3)]
    for peer in peers:
        pl.semaphore_signal(barrier, inc=1, device_id=peer, device_id_type=pl.DeviceIdType.MESH)

    load_p.wait()

    def square_step(i, acc):
        v = pv[pl.ds(pl.multiple_of(i * 16, 16), 16), :].astype(F32)
        return acc + v * v

    sq = lax.fori_loop(0, D // 16, square_step, jnp.zeros((16, KD), F32))
    scale[...] = lax.rsqrt(jnp.sum(sq, axis=0, keepdims=True) + 1e-6)

    order = [
        (Y_PLACES[i], Z_PLACES[j]) for ys, zs in GROUPS for i in range(*ys) for j in range(*zs)
    ]

    def feature_rows(row_block, dz):
        return pl.ds(pl.multiple_of((row_block * NZ + at_z(dz)) * 32, 32), 32)

    def unit_step(kb, _):
        cols = pl.ds(pl.multiple_of(kb * 128, 128), 128)
        for i in range(D // 128):
            four = order[i * 4:i * 4 + 4]
            block = jnp.concatenate([pv[feature_rows(at_y(dy), dz), cols] for dy, dz in four], axis=0)
            ut[cols, i * 128:(i + 1) * 128] = (block.astype(F32) * scale[:, cols]).T.astype(BF16)
        return 0

    lax.fori_loop(0, KD // 128, unit_step, 0)
    load_f.wait()
    pl.semaphore_wait(barrier, len(peers))

    sends = []

    def copy(src, dst, ssem, rsem, to):
        return pltpu.make_async_remote_copy(
            src_ref=src, dst_ref=dst, send_sem=ssem, recv_sem=rsem, device_id=to, device_id_type=pl.DeviceIdType.MESH
        )

    def send(src, dst, ssem, rsem, to):
        cp = copy(src, dst, ssem, rsem, to)
        cp.start()
        sends.append(cp)

    def flush(count):
        for cp in sends[:count]:
            cp.wait_send()
        del sends[:count]

    def arrived(dst, ssem, rsem):
        copy(dst, dst, ssem, rsem, dev(dc=1)).wait_recv()

    def part_of(ys, zs, core=None):
        return ft.at[:, ys[0]:ys[1], zs[0]:zs[1], c if core is None else core]

    def to_sibling(kind, ys, q):
        send(part_of(ys, STEPS[q]), part_of(ys, STEPS[q]), c_s.at[kind, q], c_r.at[kind, q], dev(dc=1))

    def from_sibling(kind, steps):
        ys = ((0, 1), (1, 3), (3, 4))[kind]
        for q in steps:
            arrived(part_of(ys, STEPS[q], 1 - c), c_s.at[0, 0], c_r.at[kind, q])

    def along_y(q):
        for side, dy, place in ((0, 1, 2), (1, 3, 1)):
            send(part_of((0, 1), STEPS[q]), part_of((place, place + 1), STEPS[q]), y_s.at[side, q], y_r.at[side, q], dev(dy=dy))
        to_sibling(0, (0, 1), q)

    def half(place, q, view):
        return ft.at[view, place, STEPS[q][0]:STEPS[q][1], c]

    def pass_on_y(q):
        for side, dy, place in ((0, 1, 2), (1, 3, 1)):
            arrived(part_of((place, place + 1), STEPS[q]), y_s.at[0, 0], y_r.at[side, q])
            send(half(place, q, side), half(3, q, side), f_s.at[side, q], f_r.at[side, q], dev(dy=dy))
        to_sibling(1, (1, 3), q)

    def from_z(q):
        for j in range(*STEPS[q]):
            arrived(part_of((0, 1), (j, j + 1)), z_s.at[0], z_r.at[Z_PLACES[j]])
        along_y(q)

    def opposite(q):
        for side in range(2):
            arrived(half(3, q, side), f_s.at[0, 0], f_r.at[side, q])
        to_sibling(2, (3, 4), q)

    def group_dot(g, v, bb):
        lanes = pl.ds(pl.multiple_of(bb * LANES, LANES), LANES)
        ys, zs = GROUPS[g]
        rhs = ft[v, ys[0]:ys[1], zs[0]:zs[1], :, :, lanes].reshape(CHUNK, LANES)
        return lanes, jnp.dot(ut[:, g * CHUNK:(g + 1) * CHUNK], rhs, preferred_element_type=F32)

    def group_scores(g, v):
        def step(bb, _):
            lanes, d = group_dot(g, v, bb)
            if g == 0:
                sc[v, :, lanes] = d
            else:
                sc[v, :, lanes] += d
            return 0

        lax.fori_loop(0, BLOCKS, step, 0)

    def group_squares(g):
        def step(bb, _):
            lanes = pl.ds(pl.multiple_of(bb * 128, 128), 128)
            for v in range(VIEWS):
                ys, zs = GROUPS[g]
                val = ft[v, ys[0]:ys[1], zs[0]:zs[1], :, :, lanes].astype(F32)
                total = jnp.sum((val * val).reshape(CHUNK, 128), axis=0, keepdims=True)
                rscale[v, :, lanes] = total if g == 0 else rscale[v, :, lanes] + total
            return 0

        lax.fori_loop(0, RD // 128, step, 0)

    along_y(0)
    for dz in z_order:
        place = Z_PLACES.index(NZ - dz)
        send(part_of((0, 1), (0, 1)), part_of((0, 1), (place, place + 1)), z_s.at[dz], z_r.at[NZ - dz], dev(dz=dz))
    from_z(1)
    pass_on_y(0)
    opposite(0)
    from_z(2)
    pass_on_y(1)
    from_z(3)
    from_z(4)
    opposite(1)
    pass_on_y(2)
    from_sibling(0, range(5))
    group_scores(0, 0)
    group_scores(0, 1)
    pass_on_y(3)
    from_sibling(1, range(3))
    group_scores(1, 0)
    pass_on_y(4)
    group_scores(1, 1)
    opposite(2)
    group_squares(0)
    group_squares(1)
    from_sibling(1, range(3, 5))
    opposite(3)
    group_scores(2, 0)
    opposite(4)
    group_scores(2, 1)
    group_squares(2)
    from_sibling(2, range(5))
    group_squares(3)
    for v in range(VIEWS):
        rscale[v] = lax.rsqrt(rscale[v] + 1e-6)

    def lane_sum_row(tiles):
        return jnp.sum(tiles.T, axis=0, keepdims=True)

    def column(buf, v, kb):
        return jnp.broadcast_to(buf[v, pl.ds(kb, 1), :], (128, 128)).T

    def sum_slots(buf, order):
        total = buf[order[0]]
        for i in order[1:]:
            total = total + buf[i]
        return total

    def last_scores(v):
        def step(bb, _):
            lanes, d = group_dot(3, v, bb)
            s = (sc[v, :, lanes] + d) * rscale[v, :, lanes]
            sc[v, :, lanes] = s
            e = jnp.exp2(s * EXP2_SCALE)
            k = e * e
            kn[v, :, lanes] = k
            mass[...] += k[:, 0:128] + k[:, 128:256]
            for j in range(LANES // 128):
                tot[v, pl.ds(bb * 2 + j, 1), :] = jnp.sum(e[:, j * 128:(j + 1) * 128], axis=0, keepdims=True)
            return 0

        mass[...] = jnp.zeros_like(mass)
        for bb in range(BLOCKS):
            step(bb, 0)
        for i in range(KD // 128):
            xbuf[0, v, 0, i:i + 1, :] = lane_sum_row(mass[i * 128:(i + 1) * 128, :])

    def proto_mass(t, v):
        def step(i, _):
            for kb in (i * 2, i * 2 + 1):
                rows = pl.ds(pl.multiple_of(kb * 128, 128), 128)
                total = kn[v, rows, 0:128] * part[0, v, 0:1, :]
                for j in range(1, RD // 128):
                    total = total + kn[v, rows, j * 128:(j + 1) * 128] * part[0, v, j:j + 1, :]
                xbuf[t, v, 0, pl.ds(kb, 1), :] = lane_sum_row(total)
            return 0

        for i in range(KD // 256):
            step(i, 0)

    def send_x(t, v):
        for dx in (2, 1, 3):
            send(xbuf.at[t, v, 0], xbuf.at[t, v, NX - dx], xs_s.at[t, v, dx], xs_r.at[t, v, NX - dx], dev(dx=dx))

    def sample_mass(t, v):
        for dx in (1, 3, 2):
            arrived(xbuf.at[t, v, dx], xs_s.at[t, v, dx], xs_r.at[t, v, dx])
        part[1, v] = 1.0 / sum_slots(xbuf.at[t, v], range(NX))

        def step(i, acc):
            for kb in (i * 2, i * 2 + 1):
                rows = pl.ds(pl.multiple_of(kb * 128, 128), 128)
                col = column(part.at[1], v, kb)
                acc = tuple(
                    acc[j] + jnp.sum((kn[v, rows, j * 128:(j + 1) * 128] * col).reshape(16, 8, 128), axis=0)
                    for j in range(RD // 128)
                )
            return acc

        acc = (jnp.zeros((8, 128), F32),) * 8
        for i in range(KD // 256):
            acc = step(i, acc)
        for j in range(RD // 128):
            ybuf[t, v, 0, 0, j:j + 1, :] = jnp.sum(acc[j], axis=0, keepdims=True)
        if t == 0:
            ybuf[t, v, 0, 1] = tot[v]

    def send_y(t, v):
        n = 2 if t == 0 else 1
        for i, (dy, dc) in enumerate(yc_peers):
            j = yc_peers.index(((-dy) % NY, dc))
            send(ybuf.at[t, v, 0, 0:n], ybuf.at[t, v, 1 + j, 0:n], ys_s.at[t, v, i], ys_r.at[t, v, j], dev(dy=dy, dc=dc))

    def send_z(t, v):
        n = 2 if t == 0 else 1
        for i in range(len(yc_peers)):
            arrived(ybuf.at[t, v, 1 + i, 0:n], ys_s.at[t, v, i], ys_r.at[t, v, i])
        zbuf[t, v, 0, 0:n] = sum_slots(ybuf.at[t, v, :, 0:n], range(8))
        for dz in z_far:
            send(zbuf.at[t, v, 0, 0:n], zbuf.at[t, v, NZ - dz, 0:n], zs_s.at[t, v, dz], zs_r.at[t, v, NZ - dz], dev(dz=dz))

    def take_z(t, v):
        n = 2 if t == 0 else 1
        for dz in z_order:
            arrived(zbuf.at[t, v, dz, 0:n], zs_s.at[t, v, dz], zs_r.at[t, v, dz])
        sums = sum_slots(zbuf.at[t, v, :, 0:n], range(NZ))
        part[0, v] = 1.0 / sums[0]
        if t == 0:
            tot[v] = sums[1]

    def predict(v):
        def step(i, _):
            rows = pl.ds(pl.multiple_of(i * 128, 128), 128)
            for j in range(RD // 128):
                lanes = slice(j * 128, (j + 1) * 128)
                weight = rscale[v, :, lanes] * HEAT / tot[v, j:j + 1, :]
                pred[v, rows, lanes] = jnp.exp2(sc[v, rows, lanes] * EXP2_SCALE) * weight
            return 0

        lax.fori_loop(0, KD // 128, step, 0)

    for t in range(ITERS):
        older = len(sends)
        for v in range(VIEWS):
            if t == 0:
                last_scores(v)
            else:
                take_z(t - 1, v)
                proto_mass(t, v)
            send_x(t, v)
        flush(older)
        for v in range(VIEWS):
            sample_mass(t, v)
            send_y(t, v)
        for v in range(VIEWS):
            send_z(t, v)
        if t:
            predict(t - 1)
    for v in range(VIEWS):
        take_z(ITERS - 1, v)

    older = len(sends)

    factor, proto_factor = part.at[0], part.at[1]
    loss_acc = jnp.zeros((8, 128), F32)
    for v in range(VIEWS):
        loss_acc += jnp.log(tot[v]) * factor[1 - v] * ybuf[ITERS - 1, 1 - v, 0, 0]
    loss_acc = -loss_acc

    def y_place(row_block):
        dy = lax.rem(row_block + NY - y, NY)
        return dy + lax.div(dy, 2) * (5 - 2 * dy)

    def grad_block(dx, cols):
        out = None
        for v in range(VIEWS):
            lhs = ft[v, y_place(at_x(dx))].reshape(CHUNK, RD)
            d = lax.dot_general(lhs, sg[v, cols, :], NT, preferred_element_type=F32)
            out = d if out is None else out + d
        return out

    def weigh(dx, cols, delta):
        own = jnp.concatenate([pv[feature_rows(at_x(dx), dz), cols] for dz in Z_PLACES], axis=0)
        return jnp.sum(own.astype(F32) * delta, axis=0, keepdims=True)

    for kc in range(CHUNKS):
        cols = slice(kc * CHUNK, (kc + 1) * CHUNK)

        def slope_step(i, acc, kc=kc):
            kb = kc * 2 + i
            rows = pl.ds(pl.multiple_of(kb * 128, 128), 128)
            for v in range(VIEWS):
                col = column(proto_factor, 1 - v, kb)
                for j in range(RD // 128):
                    lanes = slice(j * 128, (j + 1) * 128)
                    heated = rscale[v, :, lanes] * HEAT
                    s = sc[v, rows, lanes]
                    assign = kn[1 - v, rows, lanes] * col * factor[1 - v, j:j + 1, :]
                    sg[v, rows, lanes] = (pred[v, rows, lanes] - assign * heated).astype(BF16)
                    acc = acc + jnp.sum((assign * s).reshape(16, 8, 128), axis=0) * HEAT
            return acc

        loss_acc = slope_step(1, slope_step(0, loss_acc))
        delta = grad_block(2, cols)
        snd2[:, cols] = delta.astype(BF16)
        inner[0, :, cols] = weigh(2, cols, delta)
        send(snd2.at[0:128, cols], r1p.at[:, cols], h_s.at[0, kc], h_r.at[0, kc], dev(dx=1))
        send(snd2.at[128:256, cols], r1m.at[:, cols], h_s.at[1, kc], h_r.at[1, kc], dev(dx=3))

    ly[me_slot(y, c)] = loss_acc
    for i, (dy, dc) in enumerate(yc_peers):
        j = yc_peers.index(((-dy) % NY, dc))
        send(ly.at[me_slot(y, c)], ly.at[me_slot(y, c)], ly_s.at[i], ly_r.at[j], dev(dy=dy, dc=dc))

    for kc in range(CHUNKS):
        cols = slice(kc * CHUNK, (kc + 1) * CHUNK)
        dplus = grad_block(1, cols)
        dp[:, cols] = dplus
        sndp[128:256, cols] = dplus[128:256].astype(BF16)
        send(sndp.at[128:256, cols], recp.at[128:256, cols], d_s.at[0, kc], d_r.at[0, kc], dev(dx=1))
        dminus = grad_block(3, cols)
        dm[:, cols] = dminus
        sndm[0:128, cols] = dminus[0:128].astype(BF16)
        send(sndm.at[0:128, cols], recm.at[0:128, cols], d_s.at[1, kc], d_r.at[1, kc], dev(dx=3))
        own = grad_block(0, cols)
        down[:, cols] = own
        inner[0, :, cols] += weigh(1, cols, dplus) + weigh(3, cols, dminus) + weigh(0, cols, own)
    flush(older)
    older = len(sends)
    for dx in (1, 2, 3):
        send(inner.at[0], inner.at[NX - dx], in_s.at[dx], in_r.at[NX - dx], dev(dx=dx))

    for i, (dy, dc) in enumerate(yc_peers):
        slot = me_slot(at_y(dy), lax.rem(c + dc, NC))
        arrived(ly.at[slot], ly_s.at[i], ly_r.at[i])
    lz[z] = sum_slots(ly, range(8))
    for dz in z_order:
        send(lz.at[z], lz.at[z], lz_s.at[dz], lz_r.at[NZ - dz], dev(dz=dz))

    for kc in range(CHUNKS):
        cols = slice(kc * CHUNK, (kc + 1) * CHUNK)
        arrived(r1p.at[:, cols], h_s.at[0, kc], h_r.at[0, kc])
        sndp[0:128, cols] = (dp[0:128, cols] + r1p[:, cols].astype(F32)).astype(BF16)
        send(sndp.at[0:128, cols], recp.at[0:128, cols], e_s.at[0, kc], e_r.at[0, kc], dev(dx=1))
        arrived(r1m.at[:, cols], h_s.at[1, kc], h_r.at[1, kc])
        sndm[128:256, cols] = (dm[128:256, cols] + r1m[:, cols].astype(F32)).astype(BF16)
        send(sndm.at[128:256, cols], recm.at[128:256, cols], e_s.at[1, kc], e_r.at[1, kc], dev(dx=3))

    flush(older)
    older = len(sends)
    for dz in z_order:
        arrived(lz.at[at_z(dz)], lz_s.at[dz], lz_r.at[dz])
    lx[xi] = sum_slots(lz, range(NZ))
    for dx in (1, 2, 3):
        send(lx.at[xi], lx.at[xi], lx_s.at[dx], lx_r.at[NX - dx], dev(dx=dx))

    for dx in (1, 2, 3):
        arrived(inner.at[dx], in_s.at[dx], in_r.at[dx])
    weights = sum_slots(inner, range(NX)) * scale[...] * scale[...]

    for kc in range(CHUNKS):
        cols = slice(kc * CHUNK, (kc + 1) * CHUNK)
        arrived(recp.at[128:256, cols], d_s.at[0, kc], d_r.at[0, kc])
        arrived(recm.at[0:128, cols], d_s.at[1, kc], d_r.at[1, kc])
        arrived(recp.at[0:128, cols], e_s.at[0, kc], e_r.at[0, kc])
        arrived(recm.at[128:256, cols], e_s.at[1, kc], e_r.at[1, kc])
        delta = down[:, cols] + recp[:, cols].astype(F32) + recm[:, cols].astype(F32)
        for j, dz in enumerate(Z_PLACES):
            unit = pv[feature_rows(xi, dz), cols].astype(F32) * weights[:, cols]
            grad_ref[feature_rows(0, dz), cols] = scale[:, cols] * (delta[j * 32:(j + 1) * 32] - unit)

    flush(older)
    for dx in (1, 2, 3):
        arrived(lx.at[at_x(dx)], lx_s.at[dx], lx_r.at[dx])
    loss_ref[0, 0] = jnp.sum(sum_slots(lx, range(NX))) * (-1.0 / (2.0 * ROWS))

    flush(len(sends))


def me_slot(y, c):
    return y * NC + c


def per_device(features, prototypes):
    vmem = pltpu.VMEM
    dma = pltpu.SemaphoreType.DMA
    grad, loss = pl.pallas_call(
        kernel,
        out_shape=(pltpu.VMEM((CHUNK, KD), F32), jax.ShapeDtypeStruct((1, 1), F32)),
        in_specs=[pl.BlockSpec(memory_space=pl.ANY)] * 2,
        out_specs=(pl.BlockSpec(memory_space=pltpu.VMEM), pl.BlockSpec(memory_space=pltpu.SMEM)),
        scratch_shapes=[
            vmem((VIEWS, NY, NZ, NC, PIECE, RD), BF16),
            vmem((D, KD), BF16),
            vmem((KD, D), BF16),
            vmem((VIEWS, KD, RD), F32),
            vmem((VIEWS, KD, RD), F32),
            vmem((VIEWS, KD, RD), F32),
            vmem((VIEWS, KD, RD), BF16),
            vmem((1, KD), F32),
            vmem((VIEWS, 1, RD), F32),
            vmem((VIEWS, 8, 128), F32),
            vmem((2, VIEWS, 8, 128), F32),
            vmem((ITERS, VIEWS, NX, 8, 128), F32),
            vmem((ITERS, VIEWS, NY * NC, 2, 8, 128), F32),
            vmem((ITERS, VIEWS, NZ, 2, 8, 128), F32),
            vmem((KD, 128), F32),
            vmem((NX, 8, 128), F32),
            vmem((NY * NC, 8, 128), F32),
            vmem((NZ, 8, 128), F32),
            vmem((NX, 1, KD), F32),
            vmem((CHUNK, KD), BF16),
            vmem((CHUNK, KD), BF16),
            vmem((CHUNK, KD), BF16),
            vmem((CHUNK // 2, KD), BF16),
            vmem((CHUNK // 2, KD), BF16),
            vmem((CHUNK, KD), BF16),
            vmem((CHUNK, KD), BF16),
            vmem((CHUNK, KD), F32),
            vmem((CHUNK, KD), F32),
            vmem((CHUNK, KD), F32),
            dma((2,)),
            dma((NZ,)), dma((NZ,)),
            dma((2, 5)), dma((2, 5)),
            dma((2, 5)), dma((2, 5)),
            dma((3, 5)), dma((3, 5)),
            dma((ITERS, VIEWS, NX)), dma((ITERS, VIEWS, NX)),
            dma((ITERS, VIEWS, 7)), dma((ITERS, VIEWS, 7)),
            dma((ITERS, VIEWS, NZ)), dma((ITERS, VIEWS, NZ)),
            dma((NX,)), dma((NX,)),
            dma((7,)), dma((7,)),
            dma((NZ,)), dma((NZ,)),
            dma((NX,)), dma((NX,)),
            dma((2, CHUNKS)), dma((2, CHUNKS)),
            dma((2, CHUNKS)), dma((2, CHUNKS)),
            dma((2, CHUNKS)), dma((2, CHUNKS)),
        ],
        compiler_params=pltpu.CompilerParams(
            collective_id=0, has_side_effects=True, vmem_limit_bytes=56 * 2**20
        ),
    )(features.transpose(0, 2, 1), prototypes)
    return grad, loss[0, 0]


def solution(mesh):
    placed = (P(None, "batch", "proto"), P(None, "proto"))
    return jax.shard_map(
        per_device,
        mesh=mesh,
        in_specs=placed,
        out_specs=(P("batch", "proto"), P()),
        check_vma=False,
    )
```
